128 devices in a mesh: lon: 32 (over x, y, core), lat: 4 (over z).
Axes of the slice: x: 4, y: 4, z: 4, core: 2. Of those that a mesh axis runs over, the one named last changes fastest.
Arguments:
- departures: bfloat16 [524288, 128], P(('lon', 'lat')), may hold values from -8 to 8
- obs_owner: int32 [524288, 1], P(('lon', 'lat')), may hold values from 0 to 127; in each aligned block of 4096 rows (0 to 4095, 4096 to 8191, ...) at most 64 rows name the same one
- obs_cells: int32 [524288, 4], P(('lon', 'lat')), may hold values from 0 to 4095, as said below
- interp_weights: float32 [524288, 4], P(('lon', 'lat')), may hold values from 0 to 1
- inv_var: float32 [128], replicated, may hold values from 0.25 to 4
- jacobian: bfloat16 [128, 160], replicated, may hold values from -0.5 to 0.5
- face_rates: float32 [2, 128, 4096], P(None, 'lat', 'lon'), may hold values from 0.08 to 0.245
Outputs:
- gradient: float32 [160, 128, 4096], P(None, 'lat', 'lon')
The draws below stay inside these ranges and needn't reach their ends.
Inputs may be any that keep to these rules, and one draw needn't show every extreme that they name: `obs_owner`: owners are numbered lon index times the number of lat devices plus lat index. In each aligned block of 4096 rows (the rows of one device) no owner is named by more than 64 rows, a bound that some block reaches. `obs_cells`: A cell c of a tile is latitude row c // 128 and longitude column c % 128 of the owner's block.
All inputs are finite; a program needn't handle non-finite values.
Results may differ from the reference program's by a relative error of at most 0.003.
Values may be sent and summed in bfloat16 or wider, within the bound.
No kernel may reach another device: no remote copies, remote signals or barrier semaphores. Data moves between devices by JAX's collectives and lax.ppermute only.
A program may use at most 64 MiB of HBM per device.

```python
import math
import jax
import jax.numpy as jnp
import numpy as np
from jax import lax

CH = 128
STEPS = 4
CLAT = 32
CLON = 128
OBS_DEV = 4096
LEVF = 160
CAP = 64
OBS = 524288
NLAT = 128
NLON = 4096
N_LON = 32
N_LAT = 4


def draw_departures(key, part):
    key = jax.random.fold_in(key, 11)
    noise_key, common_key, amp_key = jax.random.split(key, 3)
    noise = jax.random.normal(noise_key, (OBS, CH), jnp.float32)
    amplitude = jax.random.uniform(amp_key, (OBS, 1), jnp.float32, 0.5, 1.5)
    common = jnp.clip(jax.random.normal(common_key, (1, CH), jnp.float32), -2.5, 2.5)
    return jnp.clip(noise + amplitude * common, -8.0, 8.0).astype(jnp.bfloat16)


def draw_obs_cells(key, part):
    key = jax.random.fold_in(key, 23)
    spread_key, pick_key, often_key = jax.random.split(key, 3)
    spread = jax.random.randint(spread_key, (OBS, 4), 0, CLAT * CLON, jnp.int32)
    picked = jax.random.randint(pick_key, (OBS,), 0, 4, jnp.int32)
    chosen_row = jnp.where(picked % 2 == 0, 3, CLAT - 4)
    chosen_col = jnp.where(picked // 2 == 0, 3, CLON - 4)
    chosen_cell = (chosen_row * CLON + chosen_col).astype(jnp.int32)
    frequent = jax.random.randint(often_key, (OBS,), 0, 8, jnp.int32) == 0
    first = jnp.where(frequent, chosen_cell, spread[:, 0])
    return jnp.concatenate([first[:, None], spread[:, 1:]], axis=1).astype(jnp.int32)


def draw_face_rates(key, part):
    key = jax.random.fold_in(key, 37)
    rates = jnp.exp(jax.random.uniform(key, (2, NLAT, NLON), jnp.float32, math.log(0.08), math.log(0.245)))
    return jnp.clip(rates, 0.08, 0.245).astype(jnp.float32)


def level_of(own_key, extent, cuts, least, top_value):
    def one(axis_at, shards_of):
        draws = jax.random.uniform(jax.random.fold_in(jax.random.fold_in(own_key, 6), axis_at), (shards_of,), jnp.float32, least / len(cuts), top_value / len(cuts))
        return jnp.repeat(jnp.exp(draws), extent[axis_at] // shards_of).reshape((-1,) + (1,) * (len(extent) - axis_at - 1))

    loudness = one(*cuts[0])
    for cut in cuts[1:]:
        loudness = loudness * one(*cut)
    return loudness


def deal_out(rng, own, number, rows, count, top, limit, lean):
    sequence = jax.random.permutation(rng, count)
    crowded, ordinary = load_shares(count, rows * top, limit, lean, True), load_shares(count, rows * top, limit, lean, False)
    places = jnp.arange(count)

    def named(tallies, turn):
        used = int((tallies > 0).sum())
        fixed = max(1, used // 4)
        passed = fixed + (places - fixed + turn * (used - fixed)) % max(1, count - fixed)
        return jnp.zeros((count,), jnp.int32).at[sequence[jnp.where(places < fixed, places, passed)]].set(jnp.asarray(tallies, jnp.int32))

    tallies = jnp.where(number % 4 == 0, named(crowded, number // 4), named(ordinary, number - number // 4 - 1))
    mixed = jax.random.permutation(jax.random.fold_in(own, 3), count)
    source_of, receiver = mixed[0:count // 2 * 2:2], mixed[1:count // 2 * 2:2]
    margin = jnp.minimum(tallies[source_of] - 1, limit - tallies[receiver]) // 2
    margin = jnp.where((source_of == sequence[0]) | (receiver == sequence[0]) | (tallies[receiver] == 0), 0, jnp.maximum(margin, 0))
    passed = jax.random.randint(jax.random.fold_in(own, 4), (count // 2,), 0, 1 << 20) % (margin + 1)
    tallies = tallies.at[source_of].add(-passed).at[receiver].add(passed)
    labels = jnp.searchsorted(jnp.cumsum(tallies), jnp.arange(rows * top), side="right").astype(jnp.int32)
    table = labels.reshape(top, rows).T
    table = table[jax.random.permutation(jax.random.fold_in(own, 1), rows)]
    turn = jax.random.randint(jax.random.fold_in(own, 2), (rows, 1), 0, top)
    return jnp.take_along_axis(table, (jnp.arange(top)[None, :] + turn) % top, axis=1)


def load_shares(number_of, total, reach, lean, full):
    portions = [(1 << 20) // math.isqrt(grade ** lean) + 1 for grade in range(1, number_of + 1)]
    largest = reach if full else min(reach, max(-(-total // number_of), total * portions[0] // sum(portions)))
    least = 1 if total - largest >= number_of - 1 else 0
    counts, spare = [largest] + [least] * (number_of - 1), total - largest - least * (number_of - 1)
    while spare > 0:
        free = [i for i in range(1, number_of) if counts[i] < largest] or [i for i in range(1, number_of) if counts[i] < reach]
        whole, left = sum([portions[i] for i in free]), spare
        for i in free:
            more = min(reach - counts[i], max(1, left * portions[i] // whole), spare)
            counts[i] = counts[i] + more
            spare = spare - more
    return np.array(counts)


def scatter_about(rng, shape, width, limit, kind=jnp.bfloat16):
    array = jax.random.normal(rng, shape, jnp.float32) * width
    return jnp.minimum(jnp.maximum(array, -limit), limit).astype(kind)


def setup_inputs(seed: int = 0) -> dict:
    arg_keys = jax.random.split(jax.random.key(seed), 8)
    departures = draw_departures(jax.random.fold_in(arg_keys[7], 71), 0)
    obs_owner_keys = jax.random.split(jax.random.fold_in(arg_keys[1], 1), OBS // OBS_DEV)
    obs_owner_turns = jax.random.permutation(jax.random.fold_in(arg_keys[1], 3), OBS // OBS_DEV)
    obs_owner = jax.vmap(lambda own, number: deal_out(jax.random.fold_in(arg_keys[1], 2), own, number, OBS_DEV, N_LON * N_LAT, 1, CAP, 2))(obs_owner_keys, obs_owner_turns).reshape((OBS, 1))
    obs_cells = draw_obs_cells(jax.random.fold_in(arg_keys[7], 71), 0)
    interp_weights = jnp.clip(1.0 * jax.random.uniform(arg_keys[3], (OBS, 4), jnp.float32) ** level_of(arg_keys[3], (OBS, 4), ((0, 128),), -0.2, 0.2), 0.0, 1.0)
    inv_var = jnp.clip(jnp.exp(jax.random.uniform(arg_keys[4], (CH,), jnp.float32, math.log(0.25), math.log(4.0))), 0.25, 4.0)
    jacobian = scatter_about(arg_keys[5], (CH, LEVF), CH ** -0.5, 0.5)
    face_rates = draw_face_rates(jax.random.fold_in(arg_keys[7], 71), 0)
    return {"departures": departures, "obs_owner": obs_owner, "obs_cells": obs_cells, "interp_weights": interp_weights, "inv_var": inv_var, "jacobian": jacobian, "face_rates": face_rates}


def diffuse(field, rate_x, rate_y):
    flux_x = rate_x * (jnp.roll(field, -1, 1) - field)
    flux_y = rate_y * (jnp.roll(field, -1, 0) - field)
    return field + flux_x - jnp.roll(flux_x, 1, 1) + flux_y - jnp.roll(flux_y, 1, 0)


def reference(departures, obs_owner, obs_cells, interp_weights, inv_var, jacobian, face_rates):
    scaled = (departures.astype(jnp.float32) * inv_var[None, :]).astype(jnp.bfloat16)
    profile = jnp.dot(scaled, jacobian, preferred_element_type=jnp.float32).astype(jnp.bfloat16)
    lat_rows = CLAT * N_LAT
    lon_cols = CLON * N_LON
    owner = obs_owner[:, 0]
    lon_index = owner // N_LAT
    lat_index = owner % N_LAT
    cell_row = obs_cells // CLON
    cell_col = obs_cells % CLON
    flat_cells = ((lat_index[:, None] * CLAT + cell_row) * lon_cols + lon_index[:, None] * CLON + cell_col).reshape(-1).astype(jnp.int32)
    kappa_x = face_rates[0]
    kappa_y = face_rates[1]
    rate_x = 0.5 * (kappa_x + jnp.roll(kappa_x, -1, 1))
    inside = (jnp.arange(lat_rows) < lat_rows - 1).astype(jnp.float32)
    rate_y = 0.5 * (kappa_y + jnp.roll(kappa_y, -1, 0)) * inside[:, None]

    def one_level(column):
        spread = (interp_weights * column[:, None]).reshape(-1)
        field = jnp.zeros((lat_rows * lon_cols,), jnp.float32).at[flat_cells].add(spread)
        field = field.reshape(lat_rows, lon_cols)
        for sweep in range(STEPS):
            field = diffuse(field, rate_x, rate_y)
        return field

    return lax.map(one_level, profile.astype(jnp.float32).T)
```

```python
import functools

import jax
import jax.numpy as jnp
from jax import lax
from jax.experimental import pallas as pl
from jax.experimental.pallas import tpu as pltpu
from jax.sharding import PartitionSpec as P

STEPS = 4
LANES = 128
META = 8
PAD = 8
F32 = jnp.float32
BF16 = jnp.bfloat16
VMEM_LIMIT = 56 * 1024 * 1024


def iota(shape, dim):
    return lax.broadcasted_iota(jnp.int32, shape, dim)


def pack_kernel(cap, owner_ref, cells_ref, weights_ref, rows_ref, out_ref, xd, xm, yd, ym, slots_v, slots_s, sem):
    groups = owner_ref.shape[0]
    slots = yd.shape[0]
    owner_id = iota((LANES, LANES), 0)
    before = (iota((LANES, 2 * LANES), 0) < iota((LANES, 2 * LANES), 1)).astype(F32).astype(BF16)

    def rank_group(g, base):
        own = owner_ref[pl.ds(g, 1), :]
        hit = (own == owner_id).astype(F32)
        seen = jnp.dot(hit.astype(BF16), before, preferred_element_type=F32)
        rank = jnp.sum(hit * (seen[:, :LANES] + base), axis=0, keepdims=True)
        slots_v[pl.ds(g, 1), :] = own * cap + rank.astype(jnp.int32)
        return base + seen[:, LANES:]

    lax.fori_loop(0, groups, rank_group, jnp.zeros((LANES, LANES), F32), unroll=4)
    copy = pltpu.make_async_copy(slots_v, slots_s, sem)
    copy.start()

    def stage(g, _):
        at = pl.ds(pl.multiple_of(g * LANES, LANES), LANES)
        xd[at, :] = rows_ref[at, :].astype(F32)
        cells = cells_ref[:, at]
        weights = weights_ref[:, at]
        c = [cells[k : k + 1] for k in range(4)]
        w = [weights[k : k + 1] for k in range(4)]
        merged = []
        for k in range(4):
            total = w[k]
            for m in range(k + 1, 4):
                total = total + jnp.where(c[m] == c[k], w[m], 0.0)
            for m in range(k):
                total = jnp.where(c[m] == c[k], 0.0, total)
            merged.append(total)
        row = (cells >> 7).astype(F32)
        col = (cells & 127).astype(F32)
        block = jnp.concatenate([row, col] + merged + [jnp.zeros((LANES - 12, LANES), F32)], axis=0)
        xm[at, :] = block.T
        return 0

    lax.fori_loop(0, groups, stage, 0, unroll=2)

    def clear(g, _):
        at = pl.ds(pl.multiple_of(g * LANES, LANES), LANES)
        yd[at, :] = jnp.zeros((LANES, LANES), F32)
        ym[at, :] = jnp.zeros((LANES, LANES), F32)
        return 0

    lax.fori_loop(0, slots // LANES, clear, 0, unroll=2)
    copy.wait()

    def move(g, _):
        first = pl.multiple_of(g * LANES, LANES)
        for u in range(LANES):
            s = slots_s[g, u]
            yd[pl.ds(s, 1), :] = xd[pl.ds(first + u, 1), :]
            ym[pl.ds(s, 1), :] = xm[pl.ds(first + u, 1), :]
        return 0

    lax.fori_loop(0, groups, move, 0)

    pick = (iota((16, LANES), 0) == iota((16, LANES), 1)).astype(F32).astype(BF16)
    left = iota((META, LANES), 1) < cap
    step = 2 * (cap + META)

    def emit(a, _):
        at = pl.ds(pl.multiple_of(a * LANES, LANES), LANES)
        data = yd[at, :]
        meta = lax.dot_general(
            pick, ym[at, :].astype(BF16), (((1,), (1,)), ((), ())), preferred_element_type=F32
        )
        low, high = meta[:META], meta[META:]
        first = jnp.where(left, low, pltpu.roll(high, cap, 1))
        second = jnp.where(left, pltpu.roll(low, cap, 1), high)
        block = jnp.concatenate([data[:cap], first, data[cap:], second], axis=0)
        out_ref[pl.ds(pl.multiple_of(a * step, 16), step), :] = block.astype(BF16)
        return 0

    lax.fori_loop(0, slots // LANES, emit, 0, unroll=2)


def pack(owner, cells, weights, rows, devices, cap):
    count = rows.shape[0]
    slots = devices * cap
    full = pl.BlockSpec(memory_space=pltpu.VMEM)
    return pl.pallas_call(
        functools.partial(pack_kernel, cap),
        out_shape=jax.ShapeDtypeStruct((devices * (cap + META), LANES), BF16),
        in_specs=[full] * 4,
        out_specs=full,
        scratch_shapes=[
            pltpu.VMEM((count, LANES), F32),
            pltpu.VMEM((count, LANES), F32),
            pltpu.VMEM((slots, LANES), F32),
            pltpu.VMEM((slots, LANES), F32),
            pltpu.VMEM((count // LANES, LANES), jnp.int32),
            pltpu.SMEM((count // LANES, LANES), jnp.int32),
            pltpu.SemaphoreType.DMA,
        ],
        compiler_params=pltpu.CompilerParams(vmem_limit_bytes=VMEM_LIMIT),
        cost_estimate=pl.CostEstimate(flops=4_000_000_000, bytes_accessed=40_000_000, transcendentals=0),
        name="pack",
    )(owner.reshape(count // LANES, LANES), cells.T, weights.T, rows)


def scatter_kernel(
    cap, lat_rows, recv_ref, field_ref, south_ref, north_ref, west_ref, east_ref, corner_ref, rows, meta, side
):
    slots = rows.shape[0]
    left = iota((META, LANES), 1) < cap
    step = 2 * (cap + META)
    lon_cols = field_ref.shape[0] // lat_rows

    def unpack(b, _):
        block = recv_ref[pl.ds(pl.multiple_of(b * step, 16), step), :].astype(F32)
        data = jnp.concatenate([block[:cap], block[cap + META : 2 * cap + META]], axis=0)
        rows[pl.ds(pl.multiple_of(b * LANES, LANES), LANES), :] = data.astype(BF16)
        first, second = block[cap : cap + META], block[2 * cap + META :]
        meta[b] = jnp.concatenate(
            [
                jnp.where(left, first, pltpu.roll(second, cap, 1)),
                jnp.where(left, pltpu.roll(first, cap, 1), second),
            ],
            axis=0,
        )
        return 0

    lax.fori_loop(0, slots // LANES, unpack, 0, unroll=2)
    field_ref[...] = jnp.zeros_like(field_ref)
    depth = 2 * LANES
    per = 8
    col_id = iota((lon_cols, depth), 0).astype(F32)
    row_id = iota((lat_rows, depth), 0).astype(F32)

    def accumulate(t, _):
        both = jnp.concatenate([meta[2 * t], meta[2 * t + 1]], axis=1)
        data = rows[pl.ds(pl.multiple_of(t * depth, depth), depth), :]
        col, row = [], []
        for k in range(4):
            col.append((both[4 + k : 5 + k] == col_id).astype(F32).astype(BF16))
            row.append(jnp.where(both[k : k + 1] == row_id, both[8 + k : 9 + k], 0.0))
        for block in range(lat_rows // per):
            parts = []
            for i in range(block * per, block * per + per):
                total = None
                for k in range(4):
                    term = jnp.broadcast_to(row[k][i : i + 1], (lon_cols, depth)).astype(BF16) * col[k]
                    total = term if total is None else total + term
                parts.append(total)
            spread = jnp.concatenate(parts, axis=0)
            at = pl.ds(block * per * lon_cols, per * lon_cols)
            field_ref[at, :] += jnp.dot(spread, data, preferred_element_type=F32)
        return 0

    lax.fori_loop(0, slots // depth, accumulate, 0)

    wide = STEPS * lon_cols
    total = lat_rows * lon_cols
    south_ref[...] = field_ref[:wide, :].astype(BF16)
    north_ref[...] = field_ref[total - wide :, :].astype(BF16)
    for i in range(lat_rows):
        side[0, pl.ds(STEPS * i, STEPS), :] = field_ref[pl.ds(i * lon_cols, STEPS), :]
        side[1, pl.ds(STEPS * i, STEPS), :] = field_ref[pl.ds((i + 1) * lon_cols - STEPS, STEPS), :]
    west = side[0]
    east = side[1]
    west_ref[...] = west.astype(BF16)
    east_ref[...] = east.astype(BF16)
    edge = STEPS * STEPS
    corner_ref[0] = west[:edge].astype(BF16)
    corner_ref[1] = east[:edge].astype(BF16)
    corner_ref[2] = west[-edge:].astype(BF16)
    corner_ref[3] = east[-edge:].astype(BF16)


def scatter(recv, devices, cap, lat_rows, lon_cols):
    slots = devices * cap
    full = pl.BlockSpec(memory_space=pltpu.VMEM)
    wide = STEPS * lon_cols
    tall = STEPS * lat_rows
    shapes = [
        jax.ShapeDtypeStruct((lat_rows * lon_cols, LANES), F32),
        jax.ShapeDtypeStruct((wide, LANES), BF16),
        jax.ShapeDtypeStruct((wide, LANES), BF16),
        jax.ShapeDtypeStruct((tall, LANES), BF16),
        jax.ShapeDtypeStruct((tall, LANES), BF16),
        jax.ShapeDtypeStruct((4, STEPS * STEPS, LANES), BF16),
    ]
    return pl.pallas_call(
        functools.partial(scatter_kernel, cap, lat_rows),
        out_shape=shapes,
        in_specs=[full],
        out_specs=[full] * len(shapes),
        scratch_shapes=[
            pltpu.VMEM((slots, LANES), BF16),
            pltpu.VMEM((slots // LANES, 16, LANES), F32),
            pltpu.VMEM((2, tall, LANES), F32),
        ],
        compiler_params=pltpu.CompilerParams(vmem_limit_bytes=VMEM_LIMIT),
        cost_estimate=pl.CostEstimate(flops=17_000_000_000, bytes_accessed=20_000_000, transcendentals=0),
        name="scatter",
    )(recv)


def diffuse_kernel(
    lat_rows,
    field_ref,
    south_ref,
    north_ref,
    west_ref,
    east_ref,
    corner_ref,
    face_x,
    face_y,
    gain_ref,
    jac_ref,
    out_ref,
    ping,
    pong,
):
    lon_cols = field_ref.shape[0] // lat_rows
    width = lon_cols + 2 * PAD
    tall = lat_rows + 2 * STEPS
    lead = PAD - STEPS
    trail = PAD + lon_cols
    west = west_ref[...].astype(F32)
    east = east_ref[...].astype(F32)
    corner = corner_ref[...].astype(F32)
    for i in range(tall):
        if i < STEPS:
            middle = south_ref[pl.ds(i * lon_cols, lon_cols), :].astype(F32)
            before = corner[0][STEPS * i : STEPS * i + STEPS]
            after = corner[1][STEPS * i : STEPS * i + STEPS]
        elif i < STEPS + lat_rows:
            n = i - STEPS
            middle = field_ref[pl.ds(n * lon_cols, lon_cols), :]
            before = west[STEPS * n : STEPS * n + STEPS]
            after = east[STEPS * n : STEPS * n + STEPS]
        else:
            n = i - STEPS - lat_rows
            middle = north_ref[pl.ds(n * lon_cols, lon_cols), :].astype(F32)
            before = corner[2][STEPS * n : STEPS * n + STEPS]
            after = corner[3][STEPS * n : STEPS * n + STEPS]
        ping[pl.ds(i * width, PAD), :] = jnp.zeros((PAD, LANES), F32)
        ping[pl.ds(i * width + trail, PAD), :] = jnp.zeros((PAD, LANES), F32)
        ping[pl.ds(i * width + PAD, lon_cols), :] = middle
        ping[pl.ds(i * width + lead, STEPS), :] = before
        ping[pl.ds(i * width + trail, STEPS), :] = after

    def row_at(i):
        return pl.ds(pl.multiple_of(i * width, 8), width)

    for sweep in range(STEPS):
        old, new = (ping, pong) if sweep % 2 == 0 else (pong, ping)
        low, high = sweep + 1, tall - sweep - 1

        def one_row(i, carry, old=old, new=new):
            here, flux_below = carry
            above = old[row_at(i + 1), :]
            flux_y = face_y[row_at(i), :] * (above - here)
            flux_x = face_x[row_at(i), :] * (pltpu.roll(here, width - 1, 0) - here)
            new[row_at(i), :] = here + flux_x - pltpu.roll(flux_x, 1, 0) + flux_y - flux_below
            return above, flux_y

        here = old[row_at(low), :]
        start = face_y[row_at(low - 1), :] * (here - old[row_at(low - 1), :])
        lax.fori_loop(low, high, one_row, (here, start))

    last = ping if STEPS % 2 == 0 else pong
    gain = gain_ref[...]
    jac = jnp.concatenate([jac_ref[...], jac_ref[...]], axis=1)
    levels = jac_ref.shape[0]

    def project(h, _):
        pair = []
        for u in range(2):
            at = pl.multiple_of((2 * h + u + STEPS) * width + PAD, 8)
            value = last[pl.ds(at, lon_cols), :] * gain
            head = value.astype(BF16)
            rest = (value - head.astype(F32)).astype(BF16)
            pair.append(jnp.concatenate([head, rest], axis=1))
        both = jnp.concatenate(pair, axis=0)
        result = lax.dot_general(jac, both, (((1,), (1,)), ((), ())), preferred_element_type=F32)
        out_ref[pl.ds(2 * h, levels, stride=lat_rows), :] = result[:, :lon_cols]
        out_ref[pl.ds(2 * h + 1, levels, stride=lat_rows), :] = result[:, lon_cols:]
        return 0

    lax.fori_loop(0, lat_rows // 2, project, 0)


def diffuse(field, south, north, west, east, corner, face_x, face_y, inv_var, jacobian, lat_rows, lon_cols):
    full = pl.BlockSpec(memory_space=pltpu.VMEM)
    levels = jacobian.shape[1]
    tall, width = lat_rows + 2 * STEPS, lon_cols + 2 * PAD
    out = pl.pallas_call(
        functools.partial(diffuse_kernel, lat_rows),
        out_shape=jax.ShapeDtypeStruct((levels * lat_rows, lon_cols), F32),
        in_specs=[full] * 10,
        out_specs=full,
        scratch_shapes=[pltpu.VMEM((tall * width, LANES), F32)] * 2,
        compiler_params=pltpu.CompilerParams(vmem_limit_bytes=VMEM_LIMIT),
        cost_estimate=pl.CostEstimate(flops=1_000_000_000, bytes_accessed=20_000_000, transcendentals=0),
        name="diffuse",
    )(field, south, north, west, east, corner, face_x, face_y, inv_var.reshape(1, -1), jacobian.T)
    return out.reshape(levels, lat_rows, lon_cols)


def moved(value, lon_step, lat_step):
    lons, lats = lax.axis_size("lon"), lax.axis_size("lat")
    pairs = []
    for i in range(lons):
        for j in range(lats):
            if 0 <= j + lat_step < lats:
                source = ((i + lon_step) % lons) * lats + j + lat_step
                pairs.append((source, i * lats + j))
    return lax.ppermute(value, ("lon", "lat"), pairs)


def faces(face_rates):
    lat_rows, lon_cols = face_rates.shape[1:]
    width = lon_cols + 2 * PAD
    before = moved(face_rates[:, :, -STEPS:], -1, 0)
    after = moved(face_rates[:, :, :STEPS], 1, 0)
    rates = jnp.concatenate([before, face_rates, after], axis=2)
    below = moved(rates[:, -STEPS:], 0, -1)
    above = moved(rates[:, :STEPS], 0, 1)
    rates = jnp.concatenate([below, rates, above], axis=1)
    gap = PAD - STEPS
    rates = jnp.pad(rates, ((0, 0), (0, 0), (gap, gap)))
    row = lax.axis_index("lat") * lat_rows + jnp.arange(lat_rows + 2 * STEPS) - STEPS
    inside = (row >= 0) & (row < lat_rows * lax.axis_size("lat") - 1)
    face_x = 0.5 * (rates[0] + jnp.roll(rates[0], -1, 1))
    face_y = jnp.where(inside[:, None], 0.5 * (rates[1] + jnp.roll(rates[1], -1, 0)), 0.0)
    shape = ((lat_rows + 2 * STEPS) * width, LANES)
    return (
        jnp.broadcast_to(face_x.reshape(-1, 1), shape),
        jnp.broadcast_to(face_y.reshape(-1, 1), shape),
    )


def local(departures, obs_owner, obs_cells, interp_weights, inv_var, jacobian, face_rates):
    devices = lax.axis_size(("lon", "lat"))
    cap = 2 * departures.shape[0] // devices
    lat_rows, lon_cols = face_rates.shape[1:]
    face_x, face_y = faces(face_rates)
    send = pack(obs_owner, obs_cells, interp_weights, departures, devices, cap)
    recv = lax.all_to_all(
        send.reshape(devices, cap + META, LANES), ("lon", "lat"), split_axis=0, concat_axis=0, tiled=True
    ).reshape(devices * (cap + META), LANES)
    field, south, north, west, east, corner = scatter(recv, devices, cap, lat_rows, lon_cols)
    below = moved(north, 0, -1)
    above = moved(south, 0, 1)
    before = moved(east, -1, 0)
    after = moved(west, 1, 0)
    corners = jnp.stack(
        [
            moved(corner[3], -1, -1),
            moved(corner[2], 1, -1),
            moved(corner[1], -1, 1),
            moved(corner[0], 1, 1),
        ]
    )
    return diffuse(
        field, below, above, before, after, corners, face_x, face_y, inv_var, jacobian, lat_rows, lon_cols
    )


def solution(mesh):
    in_specs = (
        P(("lon", "lat"), None),
        P(("lon", "lat"), None),
        P(("lon", "lat"), None),
        P(("lon", "lat"), None),
        P(),
        P(),
        P(None, "lat", "lon"),
    )
    out_specs = P(None, "lat", "lon")
    return jax.shard_map(local, mesh=mesh, in_specs=in_specs, out_specs=out_specs, check_vma=False)
```

```python
import functools

import jax
import jax.numpy as jnp
from jax import lax
from jax.experimental import pallas as pl
from jax.experimental.pallas import tpu as pltpu
from jax.sharding import PartitionSpec as P

STEPS = 4
LANES = 128
META = 8
PAD = 8
F32 = jnp.float32
BF16 = jnp.bfloat16
VMEM_LIMIT = 56 * 1024 * 1024


def iota(shape, dim):
    return lax.broadcasted_iota(jnp.int32, shape, dim)


def pack_kernel(cap, owner_ref, cells_ref, weights_ref, rows_ref, out_ref, xd, xm, yd, ym, slots_v, slots_s, sem):
    groups = owner_ref.shape[0]
    slots = yd.shape[0]
    owner_id = iota((LANES, LANES), 0)
    before = (iota((LANES, 2 * LANES), 0) < iota((LANES, 2 * LANES), 1)).astype(F32).astype(BF16)

    def rank_group(g, base):
        own = owner_ref[pl.ds(g, 1), :]
        hit = (own == owner_id).astype(F32)
        seen = jnp.dot(hit.astype(BF16), before, preferred_element_type=F32)
        rank = jnp.sum(hit * (seen[:, :LANES] + base), axis=0, keepdims=True)
        slots_v[pl.ds(g, 1), :] = own * cap + rank.astype(jnp.int32)
        return base + seen[:, LANES:]

    lax.fori_loop(0, groups, rank_group, jnp.zeros((LANES, LANES), F32), unroll=4)
    copy = pltpu.make_async_copy(slots_v, slots_s, sem)
    copy.start()

    def stage(g, _):
        at = pl.ds(pl.multiple_of(g * LANES, LANES), LANES)
        xd[at, :] = rows_ref[at, :].astype(F32)
        cells = cells_ref[:, at]
        weights = weights_ref[:, at]
        c = [cells[k : k + 1] for k in range(4)]
        w = [weights[k : k + 1] for k in range(4)]
        merged = []
        for k in range(4):
            total = w[k]
            for m in range(k + 1, 4):
                total = total + jnp.where(c[m] == c[k], w[m], 0.0)
            for m in range(k):
                total = jnp.where(c[m] == c[k], 0.0, total)
            merged.append(total)
        row = (cells >> 7).astype(F32)
        col = (cells & 127).astype(F32)
        block = jnp.concatenate([row, col] + merged + [jnp.zeros((LANES - 12, LANES), F32)], axis=0)
        xm[at, :] = block.T
        return 0

    lax.fori_loop(0, groups, stage, 0, unroll=2)

    def clear(g, _):
        at = pl.ds(pl.multiple_of(g * LANES, LANES), LANES)
        yd[at, :] = jnp.zeros((LANES, LANES), F32)
        ym[at, :] = jnp.zeros((LANES, LANES), F32)
        return 0

    lax.fori_loop(0, slots // LANES, clear, 0, unroll=2)
    copy.wait()

    def move(g, _):
        first = pl.multiple_of(g * LANES, LANES)
        for u in range(LANES):
            s = slots_s[g, u]
            yd[pl.ds(s, 1), :] = xd[pl.ds(first + u, 1), :]
            ym[pl.ds(s, 1), :] = xm[pl.ds(first + u, 1), :]
        return 0

    lax.fori_loop(0, groups, move, 0)

    pick = (iota((16, LANES), 0) == iota((16, LANES), 1)).astype(F32).astype(BF16)
    left = iota((META, LANES), 1) < cap
    step = 2 * (cap + META)

    batch = 8

    def emit(c, _):
        first_slot = pl.multiple_of(c * batch * LANES, LANES)
        wide = ym[pl.ds(first_slot, batch * LANES), :].astype(BF16)
        metas = lax.dot_general(pick, wide, (((1,), (1,)), ((), ())), preferred_element_type=F32)
        for u in range(batch):
            data = yd[pl.ds(first_slot + u * LANES, LANES), :]
            low = metas[:META, u * LANES : (u + 1) * LANES]
            high = metas[META:, u * LANES : (u + 1) * LANES]
            first = jnp.where(left, low, pltpu.roll(high, cap, 1))
            second = jnp.where(left, pltpu.roll(low, cap, 1), high)
            block = jnp.concatenate([data[:cap], first, data[cap:], second], axis=0)
            out_ref[pl.ds(pl.multiple_of((c * batch + u) * step, 16), step), :] = block.astype(BF16)
        return 0

    lax.fori_loop(0, slots // LANES // batch, emit, 0)


def pack(owner, cells, weights, rows, devices, cap):
    count = rows.shape[0]
    slots = devices * cap
    full = pl.BlockSpec(memory_space=pltpu.VMEM)
    return pl.pallas_call(
        functools.partial(pack_kernel, cap),
        out_shape=jax.ShapeDtypeStruct((devices * (cap + META), LANES), BF16),
        in_specs=[full] * 4,
        out_specs=full,
        scratch_shapes=[
            pltpu.VMEM((count, LANES), F32),
            pltpu.VMEM((count, LANES), F32),
            pltpu.VMEM((slots, LANES), F32),
            pltpu.VMEM((slots, LANES), F32),
            pltpu.VMEM((count // LANES, LANES), jnp.int32),
            pltpu.SMEM((count // LANES, LANES), jnp.int32),
            pltpu.SemaphoreType.DMA,
        ],
        compiler_params=pltpu.CompilerParams(vmem_limit_bytes=VMEM_LIMIT),
        cost_estimate=pl.CostEstimate(flops=4_000_000_000, bytes_accessed=40_000_000, transcendentals=0),
        name="pack",
    )(owner.reshape(count // LANES, LANES), cells.T, weights.T, rows)


def one_hots(metas, lat_rows, lon_cols):
    both = jnp.concatenate(metas, axis=1)
    depth = both.shape[1]
    col_id = iota((lon_cols, depth), 0).astype(F32)
    row_id = iota((lat_rows, depth), 0).astype(F32)
    col = [(both[4 + k : 5 + k] == col_id).astype(F32) for k in range(4)]
    row = [jnp.where(both[k : k + 1] == row_id, both[8 + k : 9 + k], 0.0) for k in range(4)]
    return col, row


def spread_rows(col, row, which, lon_cols):
    parts = []
    for i in which:
        total = None
        for k in range(4):
            term = jnp.broadcast_to(row[k][i : i + 1], (lon_cols, row[k].shape[1])).astype(BF16) * col[k]
            total = term if total is None else total + term
        parts.append(total)
    return jnp.concatenate(parts, axis=0)


def edge_kernel(
    cap, lat_rows, lon_cols, recv_ref, rates_ref, rows, meta, field_ref, south_ref, north_ref, strip_ref, acc, tmp
):
    slots = rows.shape[0]
    left = iota((META, LANES), 1) < cap
    step = 2 * (cap + META)

    def unpack(b, _):
        block = recv_ref[pl.ds(pl.multiple_of(b * step, 16), step), :].astype(F32)
        data = jnp.concatenate([block[:cap], block[cap + META : 2 * cap + META]], axis=0)
        rows[pl.ds(pl.multiple_of(b * LANES, LANES), LANES), :] = data.astype(BF16)
        first, second = block[cap : cap + META], block[2 * cap + META :]
        meta[b] = jnp.concatenate(
            [
                jnp.where(left, first, pltpu.roll(second, cap, 1)),
                jnp.where(left, pltpu.roll(first, cap, 1), second),
            ],
            axis=0,
        )
        return 0

    lax.fori_loop(0, slots // LANES, unpack, 0, unroll=4)
    field_ref[...] = jnp.zeros_like(field_ref)
    acc[...] = jnp.zeros_like(acc)
    depth = 2 * LANES
    outer = list(range(STEPS)) + list(range(lat_rows - STEPS, lat_rows))
    sides = list(range(STEPS)) + list(range(lon_cols - STEPS, lon_cols))

    def accumulate(t, _):
        data = rows[pl.ds(pl.multiple_of(t * depth, depth), depth), :]
        col, row = one_hots([meta[2 * t], meta[2 * t + 1]], lat_rows, lon_cols)
        colb = [c.astype(BF16) for c in col]
        rowb = [r.astype(BF16) for r in row]
        field_ref[...] += jnp.dot(spread_rows(colb, row, outer, lon_cols), data, preferred_element_type=F32)
        parts = []
        for j in sides:
            total = None
            for k in range(4):
                term = jnp.broadcast_to(col[k][j : j + 1], (lat_rows, depth)).astype(BF16) * rowb[k]
                total = term if total is None else total + term
            parts.append(total)
        acc[...] += jnp.dot(jnp.concatenate(parts, axis=0), data, preferred_element_type=F32)
        return 0

    lax.fori_loop(0, slots // depth, accumulate, 0)
    wide = STEPS * lon_cols
    strip_ref[...] = acc[...].astype(BF16)
    tmp[...] = jnp.zeros_like(tmp)
    for ref, first, at in ((south_ref, 0, 0), (north_ref, wide, lat_rows - STEPS)):
        tmp[0:STEPS, :] = rates_ref[at : at + STEPS, :]
        tmp[STEPS : 2 * STEPS, :] = rates_ref[lat_rows + at : lat_rows + at + STEPS, :]
        ref[:wide, :] = field_ref[first : first + wide, :].astype(BF16)
        ref[wide:, :] = tmp[...].astype(BF16)


def scatter_edges(recv, rates, devices, cap, lat_rows, lon_cols):
    slots = devices * cap
    full = pl.BlockSpec(memory_space=pltpu.VMEM)
    wide = STEPS * lon_cols
    shapes = [
        jax.ShapeDtypeStruct((slots, LANES), BF16),
        jax.ShapeDtypeStruct((slots // LANES, 16, LANES), F32),
        jax.ShapeDtypeStruct((2 * wide, LANES), F32),
        jax.ShapeDtypeStruct((wide + 16, LANES), BF16),
        jax.ShapeDtypeStruct((wide + 16, LANES), BF16),
        jax.ShapeDtypeStruct((2 * STEPS * lat_rows, LANES), BF16),
    ]
    return pl.pallas_call(
        functools.partial(edge_kernel, cap, lat_rows, lon_cols),
        out_shape=shapes,
        in_specs=[full] * 2,
        out_specs=[full] * len(shapes),
        scratch_shapes=[pltpu.VMEM((2 * STEPS * lat_rows, LANES), F32), pltpu.VMEM((16, LANES), F32)],
        compiler_params=pltpu.CompilerParams(vmem_limit_bytes=VMEM_LIMIT),
        cost_estimate=pl.CostEstimate(flops=5_000_000_000, bytes_accessed=20_000_000, transcendentals=0),
        name="scatter_edges",
    )(recv, rates)


def middle_kernel(first, last, lat_rows, lon_cols, rows_ref, meta_ref, field_ref):
    field_ref[...] = jnp.zeros_like(field_ref)
    depth = 2 * LANES
    per = 6

    def accumulate(t, _):
        data = rows_ref[pl.ds(pl.multiple_of(t * depth, depth), depth), :]
        col, row = one_hots([meta_ref[2 * t], meta_ref[2 * t + 1]], lat_rows, lon_cols)
        colb = [c.astype(BF16) for c in col]
        for i in range(first, last, per):
            spread = spread_rows(colb, row, range(i, i + per), lon_cols)
            at = pl.ds((i - first) * lon_cols, per * lon_cols)
            field_ref[at, :] += jnp.dot(spread, data, preferred_element_type=F32)
        return 0

    lax.fori_loop(0, rows_ref.shape[0] // depth, accumulate, 0)


def scatter_middle(rows, meta, first, last, lat_rows, lon_cols):
    full = pl.BlockSpec(memory_space=pltpu.VMEM)
    return pl.pallas_call(
        functools.partial(middle_kernel, first, last, lat_rows, lon_cols),
        out_shape=jax.ShapeDtypeStruct(((last - first) * lon_cols, LANES), F32),
        in_specs=[full] * 2,
        out_specs=full,
        compiler_params=pltpu.CompilerParams(vmem_limit_bytes=VMEM_LIMIT),
        cost_estimate=pl.CostEstimate(flops=7_000_000_000, bytes_accessed=20_000_000, transcendentals=0),
        name="scatter_middle",
    )(rows, meta)


def turn_kernel(lat_rows, lon_cols, below_ref, above_ref, strip_ref, rates_ref, west_ref, east_ref, tall_ref, cols):
    tall = lat_rows + 2 * STEPS
    wide = STEPS * lon_cols
    below = below_ref[...].astype(F32)
    above = above_ref[...].astype(F32)
    strip = strip_ref[...].astype(F32)
    for c in range(2):
        at = c * tall
        tall_ref[at : at + STEPS, :] = below[wide + c * STEPS : wide + (c + 1) * STEPS]
        tall_ref[at + STEPS : at + STEPS + lat_rows, :] = rates_ref[c * lat_rows : (c + 1) * lat_rows, :]
        tall_ref[at + STEPS + lat_rows : at + tall, :] = above[wide + c * STEPS : wide + (c + 1) * STEPS]
    for side, ref in ((0, west_ref), (1, east_ref)):
        base = side * (lon_cols - STEPS)
        for j in range(STEPS):
            n = (side * STEPS + j) * lat_rows
            cols[pl.ds(STEPS * STEPS + j, lat_rows, stride=STEPS), :] = strip[n : n + lat_rows]
        for i in range(STEPS):
            cols[pl.ds(STEPS * i, STEPS), :] = below[i * lon_cols + base : i * lon_cols + base + STEPS]
            n = STEPS * (STEPS + lat_rows + i)
            cols[pl.ds(n, STEPS), :] = above[i * lon_cols + base : i * lon_cols + base + STEPS]
        ref[: STEPS * tall, :] = cols[...].astype(BF16)
        ref[STEPS * tall :, :] = tall_ref[...].astype(BF16)


def turn(below, above, strip, rates, lat_rows, lon_cols):
    full = pl.BlockSpec(memory_space=pltpu.VMEM)
    tall = lat_rows + 2 * STEPS
    side = jax.ShapeDtypeStruct(((STEPS + 2) * tall, LANES), BF16)
    return pl.pallas_call(
        functools.partial(turn_kernel, lat_rows, lon_cols),
        out_shape=[side, side, jax.ShapeDtypeStruct((2 * tall, LANES), F32)],
        in_specs=[full] * 4,
        out_specs=[full] * 3,
        scratch_shapes=[pltpu.VMEM((STEPS * tall, LANES), F32)],
        compiler_params=pltpu.CompilerParams(vmem_limit_bytes=VMEM_LIMIT),
        cost_estimate=pl.CostEstimate(flops=1_000_000, bytes_accessed=1_000_000, transcendentals=0),
        name="turn",
    )(below, above, strip, rates)


def diffuse_kernel(
    lat_rows,
    lon_cols,
    lat_devices,
    place_ref,
    outer_ref,
    mid1_ref,
    mid2_ref,
    below_ref,
    above_ref,
    west_ref,
    east_ref,
    rates_ref,
    gain_ref,
    jac_ref,
    out_ref,
    ping,
    pong,
    face_x,
    face_y,
    kappa,
):
    width = lon_cols + 2 * PAD
    tall = lat_rows + 2 * STEPS
    lead = PAD - STEPS
    trail = PAD + lon_cols
    half = (lat_rows - 2 * STEPS) // 2
    west = west_ref[...].astype(F32)
    east = east_ref[...].astype(F32)

    rest = jnp.zeros((LANES - tall, LANES), F32)
    for c in range(2):
        at = STEPS * tall + c * tall
        kappa[c, 0:lead, :] = jnp.zeros((lead, LANES), F32)
        kappa[c, lead:PAD, :] = jnp.concatenate([west[at : at + tall], rest], axis=0).T[LANES - STEPS :]
        kappa[c, PAD:trail, :] = jnp.concatenate([rates_ref[c * tall : (c + 1) * tall, :], rest], axis=0).T
        kappa[c, trail : trail + STEPS, :] = jnp.concatenate([east[at : at + tall], rest], axis=0).T[:STEPS]
        kappa[c, trail + STEPS :, :] = jnp.zeros((lead, LANES), F32)
    kx, ky = kappa[0], kappa[1]
    ex = 0.5 * (kx + pltpu.roll(kx, width - 1, 0))
    row = place_ref[0] * lat_rows - STEPS + iota((width, LANES), 1)
    inside = (row >= 0) & (row < lat_rows * lat_devices - 1)
    ny = jnp.where(inside, 0.5 * (ky + pltpu.roll(ky, LANES - 1, 1)), 0.0)
    for i in range(tall):
        at = pl.ds(i * width, width)
        face_x[at, :] = jnp.broadcast_to(ex[:, i : i + 1], (width, LANES))
        face_y[at, :] = jnp.broadcast_to(ny[:, i : i + 1], (width, LANES))

    for i in range(tall):
        n = i - STEPS
        if n < 0:
            middle = below_ref[pl.ds(i * lon_cols, lon_cols), :].astype(F32)
        elif n < STEPS:
            middle = outer_ref[pl.ds(n * lon_cols, lon_cols), :]
        elif n < STEPS + half:
            middle = mid1_ref[pl.ds((n - STEPS) * lon_cols, lon_cols), :]
        elif n < STEPS + 2 * half:
            middle = mid2_ref[pl.ds((n - STEPS - half) * lon_cols, lon_cols), :]
        elif n < lat_rows:
            middle = outer_ref[pl.ds((n - 2 * half) * lon_cols, lon_cols), :]
        else:
            middle = above_ref[pl.ds((n - lat_rows) * lon_cols, lon_cols), :].astype(F32)
        ping[pl.ds(i * width, PAD), :] = jnp.zeros((PAD, LANES), F32)
        ping[pl.ds(i * width + trail, PAD), :] = jnp.zeros((PAD, LANES), F32)
        ping[pl.ds(i * width + PAD, lon_cols), :] = middle
        ping[pl.ds(i * width + lead, STEPS), :] = west[STEPS * i : STEPS * i + STEPS]
        ping[pl.ds(i * width + trail, STEPS), :] = east[STEPS * i : STEPS * i + STEPS]

    def row_at(i):
        return pl.ds(pl.multiple_of(i * width, 8), width)

    for sweep in range(STEPS):
        old, new = (ping, pong) if sweep % 2 == 0 else (pong, ping)
        low, high = sweep + 1, tall - sweep - 1

        def one_row(i, carry, old=old, new=new):
            here, flux_below = carry
            above = old[row_at(i + 1), :]
            flux_y = face_y[row_at(i), :] * (above - here)
            flux_x = face_x[row_at(i), :] * (pltpu.roll(here, width - 1, 0) - here)
            new[row_at(i), :] = here + flux_x - pltpu.roll(flux_x, 1, 0) + flux_y - flux_below
            return above, flux_y

        here = old[row_at(low), :]
        start = face_y[row_at(low - 1), :] * (here - old[row_at(low - 1), :])
        lax.fori_loop(low, high, one_row, (here, start))

    last = ping if STEPS % 2 == 0 else pong
    gain = gain_ref[...]
    jac = jnp.concatenate([jac_ref[...], jac_ref[...]], axis=1)
    levels = jac_ref.shape[0]

    def project(h, _):
        pair = []
        for u in range(2):
            at = pl.multiple_of((2 * h + u + STEPS) * width + PAD, 8)
            value = last[pl.ds(at, lon_cols), :] * gain
            head = value.astype(BF16)
            low = (value - head.astype(F32)).astype(BF16)
            pair.append(jnp.concatenate([head, low], axis=1))
        both = jnp.concatenate(pair, axis=0)
        result = lax.dot_general(jac, both, (((1,), (1,)), ((), ())), preferred_element_type=F32)
        out_ref[pl.ds(2 * h, levels, stride=lat_rows), :] = result[:, :lon_cols]
        out_ref[pl.ds(2 * h + 1, levels, stride=lat_rows), :] = result[:, lon_cols:]
        return 0

    lax.fori_loop(0, lat_rows // 2, project, 0)


def diffuse(place, outer, mid1, mid2, below, above, west, east, rates, inv_var, jacobian, lat_rows, lon_cols, lats):
    full = pl.BlockSpec(memory_space=pltpu.VMEM)
    levels = jacobian.shape[1]
    tall, width = lat_rows + 2 * STEPS, lon_cols + 2 * PAD
    out = pl.pallas_call(
        functools.partial(diffuse_kernel, lat_rows, lon_cols, lats),
        out_shape=jax.ShapeDtypeStruct((levels * lat_rows, lon_cols), F32),
        in_specs=[pl.BlockSpec(memory_space=pltpu.SMEM)] + [full] * 10,
        out_specs=full,
        scratch_shapes=[pltpu.VMEM((tall * width, LANES), F32)] * 4 + [pltpu.VMEM((2, width, LANES), F32)],
        compiler_params=pltpu.CompilerParams(vmem_limit_bytes=VMEM_LIMIT),
        cost_estimate=pl.CostEstimate(flops=1_000_000_000, bytes_accessed=20_000_000, transcendentals=0),
        name="diffuse",
    )(place, outer, mid1, mid2, below, above, west, east, rates, inv_var.reshape(1, -1), jacobian.T)
    return out.reshape(levels, lat_rows, lon_cols)


def moved(value, axis, step, wrap):
    size = lax.axis_size(axis)
    pairs = [((i + step) % size, i) for i in range(size) if wrap or 0 <= i + step < size]
    return lax.ppermute(value, axis, pairs)


def local(departures, obs_owner, obs_cells, interp_weights, inv_var, jacobian, face_rates):
    devices = lax.axis_size(("lon", "lat"))
    cap = 2 * departures.shape[0] // devices
    lat_rows, lon_cols = face_rates.shape[1:]
    rates = face_rates.reshape(2 * lat_rows, lon_cols)
    send = pack(obs_owner, obs_cells, interp_weights, departures, devices, cap)
    recv = lax.all_to_all(
        send.reshape(devices, cap + META, LANES), ("lon", "lat"), split_axis=0, concat_axis=0, tiled=True
    ).reshape(devices * (cap + META), LANES)
    rows, meta, outer, south, north, strip = scatter_edges(recv, rates, devices, cap, lat_rows, lon_cols)
    below = moved(north, "lat", -1, False)
    above = moved(south, "lat", 1, False)
    middle = lat_rows // 2
    mid1 = scatter_middle(rows, meta, STEPS, middle, lat_rows, lon_cols)
    meta, below, above = lax.optimization_barrier((meta, below, above))
    to_west, to_east, tall_rates = turn(below, above, strip, rates, lat_rows, lon_cols)
    west = moved(to_east, "lon", -1, True)
    east = moved(to_west, "lon", 1, True)
    mid2 = scatter_middle(rows, meta, middle, lat_rows - STEPS, lat_rows, lon_cols)
    place = lax.axis_index("lat").astype(jnp.int32).reshape(1)
    return diffuse(
        place,
        outer,
        mid1,
        mid2,
        below,
        above,
        west,
        east,
        tall_rates,
        inv_var,
        jacobian,
        lat_rows,
        lon_cols,
        lax.axis_size("lat"),
    )


def solution(mesh):
    in_specs = (
        P(("lon", "lat"), None),
        P(("lon", "lat"), None),
        P(("lon", "lat"), None),
        P(("lon", "lat"), None),
        P(),
        P(),
        P(None, "lat", "lon"),
    )
    out_specs = P(None, "lat", "lon")
    return jax.shard_map(local, mesh=mesh, in_specs=in_specs, out_specs=out_specs, check_vma=False)
```

```python
import functools

import jax
import jax.numpy as jnp
from jax import lax
from jax.experimental import pallas as pl
from jax.experimental.pallas import tpu as pltpu
from jax.sharding import PartitionSpec as P

STEPS = 4
LANES = 128
META = 8
PAD = 8
GROUPS = 8
TILES = 4
UNROLL_SWEEP = 1
UNROLL_PROJECT = 2
F32 = jnp.float32
BF16 = jnp.bfloat16
MIB = 1024 * 1024


def iota(shape, dim):
    return lax.broadcasted_iota(jnp.int32, shape, dim)


def pack_kernel(cap, owner_ref, cells_ref, weights_ref, rows_ref, out_ref, xd, xm, yd, ym, slots_v, slots_s, sem):
    groups = owner_ref.shape[0]
    slots = yd.shape[0]
    owner_id = iota((LANES, LANES), 0)
    before = (iota((LANES, 2 * LANES), 0) < iota((LANES, 2 * LANES), 1)).astype(F32).astype(BF16)

    def rank_group(g, base):
        own = owner_ref[pl.ds(g, 1), :]
        hit = (own == owner_id).astype(F32)
        seen = jnp.dot(hit.astype(BF16), before, preferred_element_type=F32)
        rank = jnp.sum(hit * (seen[:, :LANES] + base), axis=0, keepdims=True)
        slots_v[pl.ds(g, 1), :] = own * cap + rank.astype(jnp.int32)
        return base + seen[:, LANES:]

    lax.fori_loop(0, groups, rank_group, jnp.zeros((LANES, LANES), F32), unroll=4)
    copy = pltpu.make_async_copy(slots_v, slots_s, sem)
    copy.start()

    def stage(g, _):
        at = pl.ds(pl.multiple_of(g * LANES, LANES), LANES)
        xd[at, :] = rows_ref[at, :].astype(F32)
        cells = cells_ref[:, at]
        weights = weights_ref[:, at]
        c = [cells[k : k + 1] for k in range(4)]
        w = [weights[k : k + 1] for k in range(4)]
        merged = []
        for k in range(4):
            total = w[k]
            for m in range(k + 1, 4):
                total = total + jnp.where(c[m] == c[k], w[m], 0.0)
            for m in range(k):
                total = jnp.where(c[m] == c[k], 0.0, total)
            merged.append(total)
        row = (cells >> 7).astype(F32)
        col = (cells & 127).astype(F32)
        block = jnp.concatenate([row, col] + merged + [jnp.zeros((LANES - 12, LANES), F32)], axis=0)
        xm[at, :] = block.T
        return 0

    lax.fori_loop(0, groups, stage, 0, unroll=2)

    def clear(g, _):
        at = pl.ds(pl.multiple_of(g * LANES, LANES), LANES)
        yd[at, :] = jnp.zeros((LANES, LANES), F32)
        ym[at, :] = jnp.zeros((LANES, LANES), F32)
        return 0

    lax.fori_loop(0, slots // LANES, clear, 0, unroll=2)
    copy.wait()

    def move(g, _):
        first = pl.multiple_of(g * LANES, LANES)
        for u in range(LANES):
            s = slots_s[g, u]
            yd[pl.ds(s, 1), :] = xd[pl.ds(first + u, 1), :]
            ym[pl.ds(s, 1), :] = xm[pl.ds(first + u, 1), :]
        return 0

    lax.fori_loop(0, groups, move, 0)

    pick = (iota((16, LANES), 0) == iota((16, LANES), 1)).astype(F32).astype(BF16)
    left = iota((META, LANES), 1) < cap
    step = 2 * (cap + META)

    batch = 8

    def emit(c, _):
        first_slot = pl.multiple_of(c * batch * LANES, LANES)
        wide = ym[pl.ds(first_slot, batch * LANES), :].astype(BF16)
        metas = lax.dot_general(pick, wide, (((1,), (1,)), ((), ())), preferred_element_type=F32)
        for u in range(batch):
            data = yd[pl.ds(first_slot + u * LANES, LANES), :]
            low = metas[:META, u * LANES : (u + 1) * LANES]
            high = metas[META:, u * LANES : (u + 1) * LANES]
            first = jnp.where(left, low, pltpu.roll(high, cap, 1))
            second = jnp.where(left, pltpu.roll(low, cap, 1), high)
            block = jnp.concatenate([data[:cap], first, data[cap:], second], axis=0)
            out_ref[pl.ds(pl.multiple_of((c * batch + u) * step, 16), step), :] = block.astype(BF16)
        return 0

    lax.fori_loop(0, slots // LANES // batch, emit, 0)


def pack(owner, cells, weights, rows, devices, cap):
    count = rows.shape[0]
    slots = devices * cap
    full = pl.BlockSpec(memory_space=pltpu.VMEM)
    return pl.pallas_call(
        functools.partial(pack_kernel, cap),
        out_shape=jax.ShapeDtypeStruct((devices * (cap + META), LANES), BF16),
        in_specs=[full] * 4,
        out_specs=full,
        scratch_shapes=[
            pltpu.VMEM((count, LANES), F32),
            pltpu.VMEM((count, LANES), F32),
            pltpu.VMEM((slots, LANES), F32),
            pltpu.VMEM((slots, LANES), F32),
            pltpu.VMEM((count // LANES, LANES), jnp.int32),
            pltpu.SMEM((count // LANES, LANES), jnp.int32),
            pltpu.SemaphoreType.DMA,
        ],
        compiler_params=pltpu.CompilerParams(vmem_limit_bytes=20 * MIB),
        cost_estimate=pl.CostEstimate(flops=4_000_000_000, bytes_accessed=40_000_000, transcendentals=0),
        name="pack",
    )(owner.reshape(count // LANES, LANES), cells.T, weights.T, rows)


def column_of(lon_cols, dim_rows):
    p = iota(dim_rows, 0)
    return (p % GROUPS) * (lon_cols // GROUPS) + p // GROUPS


def one_hots(metas, lat_rows, lon_cols):
    both = jnp.concatenate(metas, axis=1)
    depth = both.shape[1]
    col_id = column_of(lon_cols, (lon_cols, depth)).astype(F32).astype(BF16)
    row_id = iota((lat_rows, depth), 0).astype(F32)
    col, row = [], []
    for k in range(4):
        apart = jnp.broadcast_to(both[4 + k : 5 + k], (16, depth)).astype(BF16)
        apart = jnp.concatenate([apart] * (lon_cols // 16), axis=0) - col_id
        col.append(jnp.maximum(1.0 - apart * apart, 0.0).astype(BF16))
        row.append(jnp.where(both[k : k + 1] == row_id, both[8 + k : 9 + k], 0.0))
    return both, col, row


def spread_rows(col, row, which, lon_cols):
    parts = []
    for i in which:
        total = None
        for k in range(4):
            term = jnp.broadcast_to(row[k][i : i + 1], (lon_cols, row[k].shape[1])).astype(BF16) * col[k]
            total = term if total is None else total + term
        parts.append(total)
    return jnp.concatenate(parts, axis=0)


def edge_kernel(
    cap, lat_rows, lon_cols, recv_ref, rates_ref, rows, meta, field_ref, south_ref, north_ref, strip_ref, acc, tmp
):
    slots = rows.shape[0]
    left = iota((META, LANES), 1) < cap
    step = 2 * (cap + META)

    def unpack(b, _):
        block = recv_ref[pl.ds(pl.multiple_of(b * step, 16), step), :].astype(F32)
        data = jnp.concatenate([block[:cap], block[cap + META : 2 * cap + META]], axis=0)
        rows[pl.ds(pl.multiple_of(b * LANES, LANES), LANES), :] = data.astype(BF16)
        first, second = block[cap : cap + META], block[2 * cap + META :]
        meta[b] = jnp.concatenate(
            [
                jnp.where(left, first, pltpu.roll(second, cap, 1)),
                jnp.where(left, pltpu.roll(first, cap, 1), second),
            ],
            axis=0,
        )
        return 0

    lax.fori_loop(0, slots // LANES, unpack, 0, unroll=4)
    field_ref[...] = jnp.zeros_like(field_ref)
    acc[...] = jnp.zeros_like(acc)
    depth = TILES * LANES
    outer = list(range(STEPS)) + list(range(lat_rows - STEPS, lat_rows))
    sides = list(range(STEPS)) + list(range(lon_cols - STEPS, lon_cols))

    def accumulate(t, _):
        data = rows[pl.ds(pl.multiple_of(t * depth, depth), depth), :]
        both, col, row = one_hots([meta[TILES * t + h] for h in range(TILES)], lat_rows, lon_cols)
        rowb = [r.astype(BF16) for r in row]
        field_ref[...] += jnp.dot(spread_rows(col, row, outer, lon_cols), data, preferred_element_type=F32)
        parts = []
        for j in sides:
            total = None
            for k in range(4):
                same = jnp.where(both[4 + k : 5 + k] == float(j), 1.0, 0.0)
                term = jnp.broadcast_to(same, (lat_rows, depth)).astype(BF16) * rowb[k]
                total = term if total is None else total + term
            parts.append(total)
        acc[...] += jnp.dot(jnp.concatenate(parts, axis=0), data, preferred_element_type=F32)
        return 0

    lax.fori_loop(0, slots // depth, accumulate, 0)
    wide = STEPS * lon_cols
    strip_ref[...] = acc[...].astype(BF16)
    tmp[...] = jnp.zeros_like(tmp)
    for ref, first, at in ((south_ref, 0, 0), (north_ref, wide, lat_rows - STEPS)):
        tmp[0:STEPS, :] = rates_ref[at : at + STEPS, :]
        tmp[STEPS : 2 * STEPS, :] = rates_ref[lat_rows + at : lat_rows + at + STEPS, :]
        ref[:wide, :] = field_ref[first : first + wide, :].astype(BF16)
        ref[wide:, :] = tmp[...].astype(BF16)


def scatter_edges(recv, rates, devices, cap, lat_rows, lon_cols):
    slots = devices * cap
    full = pl.BlockSpec(memory_space=pltpu.VMEM)
    wide = STEPS * lon_cols
    shapes = [
        jax.ShapeDtypeStruct((slots, LANES), BF16),
        jax.ShapeDtypeStruct((slots // LANES, 16, LANES), F32),
        jax.ShapeDtypeStruct((2 * wide, LANES), F32),
        jax.ShapeDtypeStruct((wide + 16, LANES), BF16),
        jax.ShapeDtypeStruct((wide + 16, LANES), BF16),
        jax.ShapeDtypeStruct((2 * STEPS * lat_rows, LANES), BF16),
    ]
    return pl.pallas_call(
        functools.partial(edge_kernel, cap, lat_rows, lon_cols),
        out_shape=shapes,
        in_specs=[full] * 2,
        out_specs=[full] * len(shapes),
        scratch_shapes=[pltpu.VMEM((2 * STEPS * lat_rows, LANES), F32), pltpu.VMEM((16, LANES), F32)],
        compiler_params=pltpu.CompilerParams(vmem_limit_bytes=14 * MIB),
        cost_estimate=pl.CostEstimate(flops=5_000_000_000, bytes_accessed=20_000_000, transcendentals=0),
        name="scatter_edges",
    )(recv, rates)


def middle_kernel(first, last, lat_rows, lon_cols, rows_ref, meta_ref, field_ref):
    field_ref[...] = jnp.zeros_like(field_ref)
    depth = TILES * LANES
    per = 4

    def accumulate(t, _):
        data = rows_ref[pl.ds(pl.multiple_of(t * depth, depth), depth), :]
        _, col, row = one_hots([meta_ref[TILES * t + h] for h in range(TILES)], lat_rows, lon_cols)
        for i in range(first, last, per):
            spread = spread_rows(col, row, range(i, i + per), lon_cols)
            at = pl.ds((i - first) * lon_cols, per * lon_cols)
            field_ref[at, :] += jnp.dot(spread, data, preferred_element_type=F32)
        return 0

    lax.fori_loop(0, rows_ref.shape[0] // depth, accumulate, 0)


def scatter_middle(rows, meta, first, last, lat_rows, lon_cols):
    full = pl.BlockSpec(memory_space=pltpu.VMEM)
    return pl.pallas_call(
        functools.partial(middle_kernel, first, last, lat_rows, lon_cols),
        out_shape=jax.ShapeDtypeStruct(((last - first) * lon_cols, LANES), F32),
        in_specs=[full] * 2,
        out_specs=full,
        compiler_params=pltpu.CompilerParams(vmem_limit_bytes=10 * MIB),
        cost_estimate=pl.CostEstimate(flops=7_000_000_000, bytes_accessed=20_000_000, transcendentals=0),
        name="scatter_middle",
    )(rows, meta)


def turn_kernel(lat_rows, lon_cols, below_ref, above_ref, strip_ref, rates_ref, west_ref, east_ref, tall_ref, cols, wide_rows):
    tall = lat_rows + 2 * STEPS
    wide = STEPS * lon_cols
    below = below_ref[...].astype(F32)
    above = above_ref[...].astype(F32)
    strip = strip_ref[...].astype(F32)
    wide_rows[0] = below
    wide_rows[1] = above
    for c in range(2):
        at = c * tall
        tall_ref[at : at + STEPS, :] = below[wide + c * STEPS : wide + (c + 1) * STEPS]
        tall_ref[at + STEPS : at + STEPS + lat_rows, :] = rates_ref[c * lat_rows : (c + 1) * lat_rows, :]
        tall_ref[at + STEPS + lat_rows : at + tall, :] = above[wide + c * STEPS : wide + (c + 1) * STEPS]
    for side, ref in ((0, west_ref), (1, east_ref)):
        first = side * (lon_cols // GROUPS - STEPS) * GROUPS + side * (GROUPS - 1)
        for j in range(STEPS):
            n = (side * STEPS + j) * lat_rows
            cols[pl.ds(STEPS * STEPS + j, lat_rows, stride=STEPS), :] = strip[n : n + lat_rows]
        for i in range(STEPS):
            picked = pl.ds(i * lon_cols + first, STEPS, stride=GROUPS)
            cols[pl.ds(STEPS * i, STEPS), :] = wide_rows[0, picked, :]
            cols[pl.ds(STEPS * (STEPS + lat_rows + i), STEPS), :] = wide_rows[1, picked, :]
        ref[: STEPS * tall, :] = cols[...].astype(BF16)
        ref[STEPS * tall :, :] = tall_ref[...].astype(BF16)


def turn(below, above, strip, rates, lat_rows, lon_cols):
    full = pl.BlockSpec(memory_space=pltpu.VMEM)
    tall = lat_rows + 2 * STEPS
    side = jax.ShapeDtypeStruct(((STEPS + 2) * tall, LANES), BF16)
    return pl.pallas_call(
        functools.partial(turn_kernel, lat_rows, lon_cols),
        out_shape=[side, side, jax.ShapeDtypeStruct((2 * tall, LANES), F32)],
        in_specs=[full] * 4,
        out_specs=[full] * 3,
        scratch_shapes=[pltpu.VMEM((STEPS * tall, LANES), F32), pltpu.VMEM((2, STEPS * lon_cols + 16, LANES), F32)],
        compiler_params=pltpu.CompilerParams(vmem_limit_bytes=3 * MIB),
        cost_estimate=pl.CostEstimate(flops=1_000_000, bytes_accessed=1_000_000, transcendentals=0),
        name="turn",
    )(below, above, strip, rates)


def diffuse_kernel(
    lat_rows,
    lon_cols,
    lat_devices,
    place_ref,
    outer_ref,
    mid1_ref,
    mid2_ref,
    below_ref,
    above_ref,
    west_ref,
    east_ref,
    rates_ref,
    gain_ref,
    jac_ref,
    out_ref,
    ping,
    pong,
    face_x,
    face_y,
    kappa,
):
    width = lon_cols + 2 * PAD
    tall = lat_rows + 2 * STEPS
    lead = PAD - STEPS
    trail = PAD + lon_cols
    half = (lat_rows - 2 * STEPS) // 2
    part = lon_cols // GROUPS
    span = (part + 2 * STEPS) * GROUPS
    west = west_ref[...].astype(F32)
    east = east_ref[...].astype(F32)

    rest = jnp.zeros((LANES - tall, LANES), F32)
    for c in range(2):
        at = STEPS * tall + c * tall
        kappa[c, 0:lead, :] = jnp.zeros((lead, LANES), F32)
        kappa[c, lead:PAD, :] = jnp.concatenate([west[at : at + tall], rest], axis=0).T[LANES - STEPS :]
        kappa[c, PAD:trail, :] = jnp.concatenate([rates_ref[c * tall : (c + 1) * tall, :], rest], axis=0).T
        kappa[c, trail : trail + STEPS, :] = jnp.concatenate([east[at : at + tall], rest], axis=0).T[:STEPS]
        kappa[c, trail + STEPS :, :] = jnp.zeros((lead, LANES), F32)

    def strips(c):
        return jnp.concatenate(
            [kappa[c, pl.ds(lead + m, GROUPS, stride=part), :] for m in range(part + 2 * STEPS)], axis=0
        )

    kx, ky = strips(0), strips(1)
    ex = 0.5 * (kx + jnp.concatenate([kx[GROUPS:], kx[:GROUPS]], axis=0))
    row = place_ref[0] * lat_rows - STEPS + iota((span, LANES), 1)
    inside = (row >= 0) & (row < lat_rows * lat_devices - 1)
    ny = jnp.where(inside, 0.5 * (ky + pltpu.roll(ky, LANES - 1, 1)), 0.0)
    for i in range(tall):
        at = pl.ds(i * span, span)
        face_x[at, :] = jnp.broadcast_to(ex[:, i : i + 1], (span, LANES))
        face_y[at, :] = jnp.broadcast_to(ny[:, i : i + 1], (span, LANES))

    strip_id = iota((GROUPS, LANES), 0)
    inner = STEPS * GROUPS
    for i in range(tall):
        n = i - STEPS
        if n < 0:
            middle = below_ref[pl.ds(i * lon_cols, lon_cols), :].astype(F32)
        elif n < STEPS:
            middle = outer_ref[pl.ds(n * lon_cols, lon_cols), :]
        elif n < STEPS + half:
            middle = mid1_ref[pl.ds((n - STEPS) * lon_cols, lon_cols), :]
        elif n < STEPS + 2 * half:
            middle = mid2_ref[pl.ds((n - STEPS - half) * lon_cols, lon_cols), :]
        elif n < lat_rows:
            middle = outer_ref[pl.ds((n - 2 * half) * lon_cols, lon_cols), :]
        else:
            middle = above_ref[pl.ds((n - lat_rows) * lon_cols, lon_cols), :].astype(F32)
        ping[pl.ds(i * span + inner, lon_cols), :] = middle
        for q in range(STEPS):
            tail = middle[(part - STEPS + q) * GROUPS : (part - STEPS + q + 1) * GROUPS]
            side = jnp.broadcast_to(west[STEPS * i + q : STEPS * i + q + 1], (GROUPS, LANES))
            before = jnp.where(strip_id == 0, side, pltpu.roll(tail, 1, 0))
            ping[pl.ds(i * span + q * GROUPS, GROUPS), :] = before
            head = middle[q * GROUPS : (q + 1) * GROUPS]
            side = jnp.broadcast_to(east[STEPS * i + q : STEPS * i + q + 1], (GROUPS, LANES))
            after = jnp.where(strip_id == GROUPS - 1, side, pltpu.roll(head, GROUPS - 1, 0))
            ping[pl.ds(i * span + inner + lon_cols + q * GROUPS, GROUPS), :] = after

    for sweep in range(STEPS):
        old, new = (ping, pong) if sweep % 2 == 0 else (pong, ping)
        low, high = sweep + 1, tall - sweep - 1
        edge = sweep * GROUPS
        count = span - 2 * edge

        def load(ref, i, edge=edge, count=count):
            return ref[pl.ds(pl.multiple_of(i * span + edge, 8), count), :]

        def one_row(i, carry, old=old, new=new, load=load, edge=edge, count=count):
            here, flux_below = carry
            above = load(old, i + 1)
            flux_y = load(face_y, i) * (above - here)
            flux_x = load(face_x, i)[: count - GROUPS] * (here[GROUPS:] - here[: count - GROUPS])
            change = flux_x[GROUPS:] - flux_x[: count - 2 * GROUPS] + (flux_y - flux_below)[GROUPS : count - GROUPS]
            at = pl.ds(pl.multiple_of(i * span + edge + GROUPS, 8), count - 2 * GROUPS)
            new[at, :] = here[GROUPS : count - GROUPS] + change
            return above, flux_y

        here = load(old, low)
        start = load(face_y, low - 1) * (here - load(old, low - 1))
        lax.fori_loop(low, high, one_row, (here, start), unroll=UNROLL_SWEEP)

    last = ping if STEPS % 2 == 0 else pong
    gain = gain_ref[...]
    jac = jnp.concatenate([jac_ref[...], jac_ref[...]], axis=1)
    levels = jac_ref.shape[0]

    def project(h, _):
        pair = []
        for u in range(2):
            at = (2 * h + u + STEPS) * span + inner
            value = jnp.concatenate([last[pl.ds(at + t, part, stride=GROUPS), :] for t in range(GROUPS)], axis=0)
            value = value * gain
            head = value.astype(BF16)
            low = (value - head.astype(F32)).astype(BF16)
            pair.append(jnp.concatenate([head, low], axis=1))
        both = jnp.concatenate(pair, axis=0)
        result = lax.dot_general(jac, both, (((1,), (1,)), ((), ())), preferred_element_type=F32)
        out_ref[pl.ds(2 * h, levels, stride=lat_rows), :] = result[:, :lon_cols]
        out_ref[pl.ds(2 * h + 1, levels, stride=lat_rows), :] = result[:, lon_cols:]
        return 0

    lax.fori_loop(0, lat_rows // 2, project, 0, unroll=UNROLL_PROJECT)


def diffuse(place, outer, mid1, mid2, below, above, west, east, rates, inv_var, jacobian, lat_rows, lon_cols, lats):
    full = pl.BlockSpec(memory_space=pltpu.VMEM)
    levels = jacobian.shape[1]
    tall, width = lat_rows + 2 * STEPS, lon_cols + 2 * PAD
    span = lon_cols + 2 * STEPS * GROUPS
    out = pl.pallas_call(
        functools.partial(diffuse_kernel, lat_rows, lon_cols, lats),
        out_shape=jax.ShapeDtypeStruct((levels * lat_rows, lon_cols), F32),
        in_specs=[pl.BlockSpec(memory_space=pltpu.SMEM)] + [full] * 10,
        out_specs=full,
        scratch_shapes=[pltpu.VMEM((tall * span, LANES), F32)] * 4 + [pltpu.VMEM((2, width, LANES), F32)],
        compiler_params=pltpu.CompilerParams(vmem_limit_bytes=28 * MIB),
        cost_estimate=pl.CostEstimate(flops=1_000_000_000, bytes_accessed=20_000_000, transcendentals=0),
        name="diffuse",
    )(place, outer, mid1, mid2, below, above, west, east, rates, inv_var.reshape(1, -1), jacobian.T)
    return out.reshape(levels, lat_rows, lon_cols)


def moved(value, axis, step, wrap):
    size = lax.axis_size(axis)
    pairs = [((i + step) % size, i) for i in range(size) if wrap or 0 <= i + step < size]
    return lax.ppermute(value, axis, pairs)


def local(departures, obs_owner, obs_cells, interp_weights, inv_var, jacobian, face_rates):
    devices = lax.axis_size(("lon", "lat"))
    cap = 2 * departures.shape[0] // devices
    lat_rows, lon_cols = face_rates.shape[1:]
    rates = face_rates.reshape(2 * lat_rows, lon_cols)
    send = pack(obs_owner, obs_cells, interp_weights, departures, devices, cap)
    recv = lax.all_to_all(
        send.reshape(devices, cap + META, LANES), ("lon", "lat"), split_axis=0, concat_axis=0, tiled=True
    ).reshape(devices * (cap + META), LANES)
    rows, meta, outer, south, north, strip = scatter_edges(recv, rates, devices, cap, lat_rows, lon_cols)
    below = moved(north, "lat", -1, False)
    above = moved(south, "lat", 1, False)
    middle = lat_rows // 2
    mid1 = scatter_middle(rows, meta, STEPS, middle, lat_rows, lon_cols)
    meta, below, above = lax.optimization_barrier((meta, below, above))
    to_west, to_east, tall_rates = turn(below, above, strip, rates, lat_rows, lon_cols)
    west = moved(to_east, "lon", -1, True)
    east = moved(to_west, "lon", 1, True)
    mid2 = scatter_middle(rows, meta, middle, lat_rows - STEPS, lat_rows, lon_cols)
    place = lax.axis_index("lat").astype(jnp.int32).reshape(1)
    return diffuse(
        place,
        outer,
        mid1,
        mid2,
        below,
        above,
        west,
        east,
        tall_rates,
        inv_var,
        jacobian,
        lat_rows,
        lon_cols,
        lax.axis_size("lat"),
    )


def solution(mesh):
    in_specs = (
        P(("lon", "lat"), None),
        P(("lon", "lat"), None),
        P(("lon", "lat"), None),
        P(("lon", "lat"), None),
        P(),
        P(),
        P(None, "lat", "lon"),
    )
    out_specs = P(None, "lat", "lon")
    return jax.shard_map(local, mesh=mesh, in_specs=in_specs, out_specs=out_specs, check_vma=False)
```

```python
import functools

import jax
import jax.numpy as jnp
from jax import lax
from jax.experimental import pallas as pl
from jax.experimental.pallas import tpu as pltpu
from jax.sharding import PartitionSpec as P

STEPS = 4
LANES = 128
META = 8
PAD = 8
GROUPS = 8
TILES = 16
CHUNKS = 8
UNROLL_RANK = 8
UNROLL_SWEEP = 6
SWEEP_PARTS = 2
UNROLL_PROJECT = 16
F32 = jnp.float32
BF16 = jnp.bfloat16
MIB = 1024 * 1024


def iota(shape, dim):
    return lax.broadcasted_iota(jnp.int32, shape, dim)


def pack_kernel(
    cap,
    owner_hbm,
    cells_hbm,
    weights_hbm,
    rows_hbm,
    out_hbm,
    owner_ref,
    cells_ref,
    weights_ref,
    rows_ref,
    out_ref,
    xd,
    xm,
    yd,
    ym,
    slots_v,
    slots_s,
    in_sems,
    slot_sems,
    out_sems,
):
    groups = owner_ref.shape[0]
    slots = yd.shape[0]
    loads = [
        pltpu.make_async_copy(src, dst, in_sems.at[n])
        for n, (src, dst) in enumerate(
            ((owner_hbm, owner_ref), (cells_hbm, cells_ref), (weights_hbm, weights_ref), (rows_hbm, rows_ref))
        )
    ]
    for load in loads:
        load.start()

    def clear(g, _):
        at = pl.ds(pl.multiple_of(g * LANES, LANES), LANES)
        yd[at, :] = jnp.zeros((LANES, LANES), F32)
        ym[at, :] = jnp.zeros((LANES, LANES), F32)
        return 0

    lax.fori_loop(0, slots // LANES, clear, 0, unroll=2)
    owner_id = iota((LANES, LANES), 0)
    before = (iota((LANES, 2 * LANES), 0) < iota((LANES, 2 * LANES), 1)).astype(F32).astype(BF16)
    for load in loads:
        load.wait()

    def rank_and_stage(g, base):
        own = owner_ref[pl.ds(g, 1), :]
        hit = (own == owner_id).astype(F32)
        seen = jnp.dot(hit.astype(BF16), before, preferred_element_type=F32)
        rank = jnp.sum(hit * (seen[:, :LANES] + base), axis=0, keepdims=True)
        slots_v[pl.ds(g, 1), :] = own * cap + rank.astype(jnp.int32)

        at = pl.ds(pl.multiple_of(g * LANES, LANES), LANES)
        xd[at, :] = rows_ref[at, :].astype(F32)
        cells = cells_ref[:, at]
        weights = weights_ref[:, at]
        c = [cells[k : k + 1] for k in range(4)]
        w = [weights[k : k + 1] for k in range(4)]
        merged = []
        for k in range(4):
            total = w[k]
            for m in range(k + 1, 4):
                total = total + jnp.where(c[m] == c[k], w[m], 0.0)
            for m in range(k):
                total = jnp.where(c[m] == c[k], 0.0, total)
            merged.append(total)
        row = (cells >> 7).astype(F32)
        col = (cells & 127).astype(F32)
        block = jnp.concatenate([row, col] + merged + [jnp.zeros((LANES - 12, LANES), F32)], axis=0)
        xm[at, :] = block.T
        return base + seen[:, LANES:]

    def move(g, _):
        first = pl.multiple_of(g * LANES, LANES)
        for u in range(LANES):
            s = slots_s[g, u]
            yd[pl.ds(s, 1), :] = xd[pl.ds(first + u, 1), :]
            ym[pl.ds(s, 1), :] = xm[pl.ds(first + u, 1), :]
        return 0

    half = groups // 2
    base = jnp.zeros((LANES, LANES), F32)
    copies = []
    for h in range(2):
        base = lax.fori_loop(h * half, (h + 1) * half, rank_and_stage, base, unroll=UNROLL_RANK)
        part = pl.ds(h * half, half)
        copies.append(pltpu.make_async_copy(slots_v.at[part], slots_s.at[part], slot_sems.at[h]))
        copies[h].start()
    for h in range(2):
        copies[h].wait()
        lax.fori_loop(h * half, (h + 1) * half, move, 0)

    pick = (iota((16, LANES), 0) == iota((16, LANES), 1)).astype(F32).astype(BF16)
    left = iota((META, LANES), 1) < cap
    step = 2 * (cap + META)
    batch = slots // LANES // CHUNKS
    stores = []
    for c in range(CHUNKS):
        first_slot = c * batch * LANES
        wide = ym[pl.ds(first_slot, batch * LANES), :].astype(BF16)
        metas = lax.dot_general(pick, wide, (((1,), (1,)), ((), ())), preferred_element_type=F32)
        for u in range(batch):
            data = yd[pl.ds(first_slot + u * LANES, LANES), :]
            low = metas[:META, u * LANES : (u + 1) * LANES]
            high = metas[META:, u * LANES : (u + 1) * LANES]
            first = jnp.where(left, low, pltpu.roll(high, cap, 1))
            second = jnp.where(left, pltpu.roll(low, cap, 1), high)
            block = jnp.concatenate([data[:cap], first, data[cap:], second], axis=0)
            out_ref[pl.ds((c * batch + u) * step, step), :] = block.astype(BF16)
        part = pl.ds(c * batch * step, batch * step)
        stores.append(pltpu.make_async_copy(out_ref.at[part], out_hbm.at[part], out_sems.at[c]))
        stores[c].start()
    for store in stores:
        store.wait()


def pack(owner, cells, weights, rows, devices, cap):
    count = rows.shape[0]
    slots = devices * cap
    groups = count // LANES
    sent = devices * (cap + META)
    hbm = pl.BlockSpec(memory_space=pltpu.HBM)
    return pl.pallas_call(
        functools.partial(pack_kernel, cap),
        out_shape=jax.ShapeDtypeStruct((sent, LANES), BF16),
        in_specs=[hbm] * 4,
        out_specs=hbm,
        scratch_shapes=[
            pltpu.VMEM((groups, LANES), jnp.int32),
            pltpu.VMEM((4, count), jnp.int32),
            pltpu.VMEM((4, count), F32),
            pltpu.VMEM((count, LANES), BF16),
            pltpu.VMEM((sent, LANES), BF16),
            pltpu.VMEM((count, LANES), F32),
            pltpu.VMEM((count, LANES), F32),
            pltpu.VMEM((slots, LANES), F32),
            pltpu.VMEM((slots, LANES), F32),
            pltpu.VMEM((groups, LANES), jnp.int32),
            pltpu.SMEM((groups, LANES), jnp.int32),
            pltpu.SemaphoreType.DMA((4,)),
            pltpu.SemaphoreType.DMA((2,)),
            pltpu.SemaphoreType.DMA((CHUNKS,)),
        ],
        compiler_params=pltpu.CompilerParams(vmem_limit_bytes=60 * MIB),
        cost_estimate=pl.CostEstimate(flops=4_000_000_000, bytes_accessed=40_000_000, transcendentals=0),
        name="pack",
    )(owner.reshape(groups, LANES), cells.T, weights.T, rows)


def column_of(lon_cols, dim_rows):
    p = iota(dim_rows, 0)
    return (p % GROUPS) * (lon_cols // GROUPS) + p // GROUPS


def one_hots(metas, lat_rows, lon_cols):
    both = jnp.concatenate(metas, axis=1)
    depth = both.shape[1]
    col_id = column_of(lon_cols, (lon_cols, depth)).astype(F32).astype(BF16)
    row_id = iota((lat_rows, depth), 0).astype(F32)
    col, row = [], []
    for k in range(4):
        apart = jnp.broadcast_to(both[4 + k : 5 + k], (16, depth)).astype(BF16)
        apart = jnp.concatenate([apart] * (lon_cols // 16), axis=0) - col_id
        col.append(jnp.maximum(1.0 - apart * apart, 0.0).astype(BF16))
        row.append(jnp.where(both[k : k + 1] == row_id, both[8 + k : 9 + k], 0.0))
    return both, col, row


def spread_rows(col, row, which, lon_cols):
    parts = []
    for i in which:
        total = None
        for k in range(4):
            term = jnp.broadcast_to(row[k][i : i + 1], (lon_cols, row[k].shape[1])).astype(BF16) * col[k]
            total = term if total is None else total + term
        parts.append(total)
    return jnp.concatenate(parts, axis=0)


def edge_kernel(
    cap, lat_rows, lon_cols, recv_ref, rates_ref, rows, meta, field_ref, south_ref, north_ref, strip_ref, acc, tmp
):
    slots = rows.shape[0]
    left = iota((META, LANES), 1) < cap
    step = 2 * (cap + META)

    def unpack(b, _):
        block = recv_ref[pl.ds(pl.multiple_of(b * step, 16), step), :].astype(F32)
        data = jnp.concatenate([block[:cap], block[cap + META : 2 * cap + META]], axis=0)
        rows[pl.ds(pl.multiple_of(b * LANES, LANES), LANES), :] = data.astype(BF16)
        first, second = block[cap : cap + META], block[2 * cap + META :]
        meta[b] = jnp.concatenate(
            [
                jnp.where(left, first, pltpu.roll(second, cap, 1)),
                jnp.where(left, pltpu.roll(first, cap, 1), second),
            ],
            axis=0,
        )
        return 0

    lax.fori_loop(0, slots // LANES, unpack, 0, unroll=4)
    field_ref[...] = jnp.zeros_like(field_ref)
    acc[...] = jnp.zeros_like(acc)
    depth = TILES * LANES
    outer = list(range(STEPS)) + list(range(lat_rows - STEPS, lat_rows))
    sides = list(range(STEPS)) + list(range(lon_cols - STEPS, lon_cols))

    def accumulate(t, _):
        data = rows[pl.ds(pl.multiple_of(t * depth, depth), depth), :]
        both, col, row = one_hots([meta[TILES * t + h] for h in range(TILES)], lat_rows, lon_cols)
        rowb = [r.astype(BF16) for r in row]
        field_ref[...] += jnp.dot(spread_rows(col, row, outer, lon_cols), data, preferred_element_type=F32)
        parts = []
        for j in sides:
            total = None
            for k in range(4):
                same = jnp.where(both[4 + k : 5 + k] == float(j), 1.0, 0.0)
                term = jnp.broadcast_to(same, (lat_rows, depth)).astype(BF16) * rowb[k]
                total = term if total is None else total + term
            parts.append(total)
        acc[...] += jnp.dot(jnp.concatenate(parts, axis=0), data, preferred_element_type=F32)
        return 0

    lax.fori_loop(0, slots // depth, accumulate, 0)
    wide = STEPS * lon_cols
    strip_ref[...] = acc[...].astype(BF16)
    tmp[...] = jnp.zeros_like(tmp)
    for ref, first, at in ((south_ref, 0, 0), (north_ref, wide, lat_rows - STEPS)):
        tmp[0:STEPS, :] = rates_ref[at : at + STEPS, :]
        tmp[STEPS : 2 * STEPS, :] = rates_ref[lat_rows + at : lat_rows + at + STEPS, :]
        ref[:wide, :] = field_ref[first : first + wide, :].astype(BF16)
        ref[wide:, :] = tmp[...].astype(BF16)


def scatter_edges(recv, rates, devices, cap, lat_rows, lon_cols):
    slots = devices * cap
    full = pl.BlockSpec(memory_space=pltpu.VMEM)
    wide = STEPS * lon_cols
    shapes = [
        jax.ShapeDtypeStruct((slots, LANES), BF16),
        jax.ShapeDtypeStruct((slots // LANES, 16, LANES), F32),
        jax.ShapeDtypeStruct((2 * wide, LANES), F32),
        jax.ShapeDtypeStruct((wide + 16, LANES), BF16),
        jax.ShapeDtypeStruct((wide + 16, LANES), BF16),
        jax.ShapeDtypeStruct((2 * STEPS * lat_rows, LANES), BF16),
    ]
    return pl.pallas_call(
        functools.partial(edge_kernel, cap, lat_rows, lon_cols),
        out_shape=shapes,
        in_specs=[full] * 2,
        out_specs=[full] * len(shapes),
        scratch_shapes=[pltpu.VMEM((2 * STEPS * lat_rows, LANES), F32), pltpu.VMEM((16, LANES), F32)],
        compiler_params=pltpu.CompilerParams(vmem_limit_bytes=14 * MIB),
        cost_estimate=pl.CostEstimate(flops=5_000_000_000, bytes_accessed=20_000_000, transcendentals=0),
        name="scatter_edges",
    )(recv, rates)


def middle_kernel(first, last, lat_rows, lon_cols, rows_ref, meta_ref, field_ref):
    field_ref[...] = jnp.zeros_like(field_ref)
    depth = TILES * LANES
    per = 4

    def accumulate(t, _):
        data = rows_ref[pl.ds(pl.multiple_of(t * depth, depth), depth), :]
        _, col, row = one_hots([meta_ref[TILES * t + h] for h in range(TILES)], lat_rows, lon_cols)
        for i in range(first, last, per):
            spread = spread_rows(col, row, range(i, i + per), lon_cols)
            at = pl.ds((i - first) * lon_cols, per * lon_cols)
            field_ref[at, :] += jnp.dot(spread, data, preferred_element_type=F32)
        return 0

    lax.fori_loop(0, rows_ref.shape[0] // depth, accumulate, 0)


def scatter_middle(rows, meta, first, last, lat_rows, lon_cols):
    full = pl.BlockSpec(memory_space=pltpu.VMEM)
    return pl.pallas_call(
        functools.partial(middle_kernel, first, last, lat_rows, lon_cols),
        out_shape=jax.ShapeDtypeStruct(((last - first) * lon_cols, LANES), F32),
        in_specs=[full] * 2,
        out_specs=full,
        compiler_params=pltpu.CompilerParams(vmem_limit_bytes=10 * MIB),
        cost_estimate=pl.CostEstimate(flops=7_000_000_000, bytes_accessed=20_000_000, transcendentals=0),
        name="scatter_middle",
    )(rows, meta)


def turn_kernel(lat_rows, lon_cols, below_ref, above_ref, strip_ref, rates_ref, west_ref, east_ref, tall_ref, cols, wide_rows):
    tall = lat_rows + 2 * STEPS
    wide = STEPS * lon_cols
    below = below_ref[...].astype(F32)
    above = above_ref[...].astype(F32)
    strip = strip_ref[...].astype(F32)
    wide_rows[0] = below
    wide_rows[1] = above
    for c in range(2):
        at = c * tall
        tall_ref[at : at + STEPS, :] = below[wide + c * STEPS : wide + (c + 1) * STEPS]
        tall_ref[at + STEPS : at + STEPS + lat_rows, :] = rates_ref[c * lat_rows : (c + 1) * lat_rows, :]
        tall_ref[at + STEPS + lat_rows : at + tall, :] = above[wide + c * STEPS : wide + (c + 1) * STEPS]
    for side, ref in ((0, west_ref), (1, east_ref)):
        first = side * (lon_cols // GROUPS - STEPS) * GROUPS + side * (GROUPS - 1)
        for j in range(STEPS):
            n = (side * STEPS + j) * lat_rows
            cols[pl.ds(STEPS * STEPS + j, lat_rows, stride=STEPS), :] = strip[n : n + lat_rows]
        for i in range(STEPS):
            picked = pl.ds(i * lon_cols + first, STEPS, stride=GROUPS)
            cols[pl.ds(STEPS * i, STEPS), :] = wide_rows[0, picked, :]
            cols[pl.ds(STEPS * (STEPS + lat_rows + i), STEPS), :] = wide_rows[1, picked, :]
        ref[: STEPS * tall, :] = cols[...].astype(BF16)
        ref[STEPS * tall :, :] = tall_ref[...].astype(BF16)


def turn(below, above, strip, rates, lat_rows, lon_cols):
    full = pl.BlockSpec(memory_space=pltpu.VMEM)
    tall = lat_rows + 2 * STEPS
    side = jax.ShapeDtypeStruct(((STEPS + 2) * tall, LANES), BF16)
    return pl.pallas_call(
        functools.partial(turn_kernel, lat_rows, lon_cols),
        out_shape=[side, side, jax.ShapeDtypeStruct((2 * tall, LANES), F32)],
        in_specs=[full] * 4,
        out_specs=[full] * 3,
        scratch_shapes=[pltpu.VMEM((STEPS * tall, LANES), F32), pltpu.VMEM((2, STEPS * lon_cols + 16, LANES), F32)],
        compiler_params=pltpu.CompilerParams(vmem_limit_bytes=3 * MIB),
        cost_estimate=pl.CostEstimate(flops=1_000_000, bytes_accessed=1_000_000, transcendentals=0),
        name="turn",
    )(below, above, strip, rates)


def diffuse_kernel(
    lat_rows,
    lon_cols,
    lat_devices,
    place_ref,
    outer_ref,
    mid1_ref,
    mid2_ref,
    below_ref,
    above_ref,
    west_ref,
    east_ref,
    rates_ref,
    gain_ref,
    jac_ref,
    out_ref,
    ping,
    pong,
    face_x,
    face_y,
    kappa,
):
    width = lon_cols + 2 * PAD
    tall = lat_rows + 2 * STEPS
    lead = PAD - STEPS
    trail = PAD + lon_cols
    half = (lat_rows - 2 * STEPS) // 2
    part = lon_cols // GROUPS
    span = (part + 2 * STEPS) * GROUPS
    west = west_ref[...].astype(F32)
    east = east_ref[...].astype(F32)

    rest = jnp.zeros((LANES - tall, LANES), F32)
    for c in range(2):
        at = STEPS * tall + c * tall
        kappa[c, 0:lead, :] = jnp.zeros((lead, LANES), F32)
        kappa[c, lead:PAD, :] = jnp.concatenate([west[at : at + tall], rest], axis=0).T[LANES - STEPS :]
        kappa[c, PAD:trail, :] = jnp.concatenate([rates_ref[c * tall : (c + 1) * tall, :], rest], axis=0).T
        kappa[c, trail : trail + STEPS, :] = jnp.concatenate([east[at : at + tall], rest], axis=0).T[:STEPS]
        kappa[c, trail + STEPS :, :] = jnp.zeros((lead, LANES), F32)

    def strips(c):
        return jnp.concatenate(
            [kappa[c, pl.ds(lead + m, GROUPS, stride=part), :] for m in range(part + 2 * STEPS)], axis=0
        )

    kx, ky = strips(0), strips(1)
    ex = 0.5 * (kx + jnp.concatenate([kx[GROUPS:], kx[:GROUPS]], axis=0))
    row = place_ref[0] * lat_rows - STEPS + iota((span, LANES), 1)
    inside = (row >= 0) & (row < lat_rows * lat_devices - 1)
    ny = jnp.where(inside, 0.5 * (ky + pltpu.roll(ky, LANES - 1, 1)), 0.0)
    for i in range(tall):
        at = pl.ds(i * span, span)
        face_x[at, :] = jnp.broadcast_to(ex[:, i : i + 1], (span, LANES))
        face_y[at, :] = jnp.broadcast_to(ny[:, i : i + 1], (span, LANES))

    strip_id = iota((GROUPS, LANES), 0)
    inner = STEPS * GROUPS
    for i in range(tall):
        n = i - STEPS
        if n < 0:
            middle = below_ref[pl.ds(i * lon_cols, lon_cols), :].astype(F32)
        elif n < STEPS:
            middle = outer_ref[pl.ds(n * lon_cols, lon_cols), :]
        elif n < STEPS + half:
            middle = mid1_ref[pl.ds((n - STEPS) * lon_cols, lon_cols), :]
        elif n < STEPS + 2 * half:
            middle = mid2_ref[pl.ds((n - STEPS - half) * lon_cols, lon_cols), :]
        elif n < lat_rows:
            middle = outer_ref[pl.ds((n - 2 * half) * lon_cols, lon_cols), :]
        else:
            middle = above_ref[pl.ds((n - lat_rows) * lon_cols, lon_cols), :].astype(F32)
        ping[pl.ds(i * span + inner, lon_cols), :] = middle
        for q in range(STEPS):
            tail = middle[(part - STEPS + q) * GROUPS : (part - STEPS + q + 1) * GROUPS]
            side = jnp.broadcast_to(west[STEPS * i + q : STEPS * i + q + 1], (GROUPS, LANES))
            before = jnp.where(strip_id == 0, side, pltpu.roll(tail, 1, 0))
            ping[pl.ds(i * span + q * GROUPS, GROUPS), :] = before
            head = middle[q * GROUPS : (q + 1) * GROUPS]
            side = jnp.broadcast_to(east[STEPS * i + q : STEPS * i + q + 1], (GROUPS, LANES))
            after = jnp.where(strip_id == GROUPS - 1, side, pltpu.roll(head, GROUPS - 1, 0))
            ping[pl.ds(i * span + inner + lon_cols + q * GROUPS, GROUPS), :] = after

    for sweep in range(STEPS):
        old, new = (ping, pong) if sweep % 2 == 0 else (pong, ping)
        low, high = sweep + 1, tall - sweep - 1
        first, stop = sweep + 1, span // GROUPS - 1 - sweep
        cuts = [first + (stop - first) * n // SWEEP_PARTS for n in range(SWEEP_PARTS + 1)]
        for at, end in zip(cuts[:-1], cuts[1:]):
            inside_rows = (end - at) * GROUPS

            def load(ref, i, start, count):
                return ref[pl.ds(pl.multiple_of(i * span + start * GROUPS, 8), count), :]

            def one_row(i, carry, old=old, new=new, at=at, count=inside_rows):
                here, flux_below = carry
                above = load(old, i + 1, at - 1, count + 2 * GROUPS)
                flux_y = load(face_y, i, at, count) * (above - here)[GROUPS : count + GROUPS]
                flux_x = load(face_x, i, at - 1, count + GROUPS) * (here[GROUPS:] - here[: count + GROUPS])
                change = flux_x[GROUPS:] - flux_x[:count] + (flux_y - flux_below)
                new[pl.ds(pl.multiple_of(i * span + at * GROUPS, 8), count), :] = here[GROUPS : count + GROUPS] + change
                return above, flux_y

            here = load(old, low, at - 1, inside_rows + 2 * GROUPS)
            start = load(old, low - 1, at, inside_rows)
            start = load(face_y, low - 1, at, inside_rows) * (here[GROUPS : inside_rows + GROUPS] - start)
            lax.fori_loop(low, high, one_row, (here, start), unroll=UNROLL_SWEEP)

    last = ping if STEPS % 2 == 0 else pong
    gain = gain_ref[...]
    jac = jnp.concatenate([jac_ref[...], jac_ref[...]], axis=1)
    levels = jac_ref.shape[0]

    def project(h, _):
        pair = []
        for u in range(2):
            at = (2 * h + u + STEPS) * span + inner
            value = jnp.concatenate([last[pl.ds(at + t, part, stride=GROUPS), :] for t in range(GROUPS)], axis=0)
            value = value * gain
            head = value.astype(BF16)
            low = (value - head.astype(F32)).astype(BF16)
            pair.append(jnp.concatenate([head, low], axis=1))
        both = jnp.concatenate(pair, axis=0)
        result = lax.dot_general(jac, both, (((1,), (1,)), ((), ())), preferred_element_type=F32)
        out_ref[pl.ds(2 * h, levels, stride=lat_rows), :] = result[:, :lon_cols]
        out_ref[pl.ds(2 * h + 1, levels, stride=lat_rows), :] = result[:, lon_cols:]
        return 0

    lax.fori_loop(0, lat_rows // 2, project, 0, unroll=UNROLL_PROJECT)


def diffuse(place, outer, mid1, mid2, below, above, west, east, rates, inv_var, jacobian, lat_rows, lon_cols, lats):
    full = pl.BlockSpec(memory_space=pltpu.VMEM)
    levels = jacobian.shape[1]
    tall, width = lat_rows + 2 * STEPS, lon_cols + 2 * PAD
    span = lon_cols + 2 * STEPS * GROUPS
    out = pl.pallas_call(
        functools.partial(diffuse_kernel, lat_rows, lon_cols, lats),
        out_shape=jax.ShapeDtypeStruct((levels * lat_rows, lon_cols), F32),
        in_specs=[pl.BlockSpec(memory_space=pltpu.SMEM)] + [full] * 10,
        out_specs=full,
        scratch_shapes=[pltpu.VMEM((tall * span, LANES), F32)] * 4 + [pltpu.VMEM((2, width, LANES), F32)],
        compiler_params=pltpu.CompilerParams(vmem_limit_bytes=28 * MIB),
        cost_estimate=pl.CostEstimate(flops=1_000_000_000, bytes_accessed=20_000_000, transcendentals=0),
        name="diffuse",
    )(place, outer, mid1, mid2, below, above, west, east, rates, inv_var.reshape(1, -1), jacobian.T)
    return out.reshape(levels, lat_rows, lon_cols)


def moved(value, axis, step, wrap):
    size = lax.axis_size(axis)
    pairs = [((i + step) % size, i) for i in range(size) if wrap or 0 <= i + step < size]
    return lax.ppermute(value, axis, pairs)


def local(departures, obs_owner, obs_cells, interp_weights, inv_var, jacobian, face_rates):
    devices = lax.axis_size(("lon", "lat"))
    cap = 2 * departures.shape[0] // devices
    lat_rows, lon_cols = face_rates.shape[1:]
    rates = face_rates.reshape(2 * lat_rows, lon_cols)
    send = pack(obs_owner, obs_cells, interp_weights, departures, devices, cap)
    recv = lax.all_to_all(
        send.reshape(devices, cap + META, LANES), ("lon", "lat"), split_axis=0, concat_axis=0, tiled=True
    ).reshape(devices * (cap + META), LANES)
    rows, meta, outer, south, north, strip = scatter_edges(recv, rates, devices, cap, lat_rows, lon_cols)
    below = moved(north, "lat", -1, False)
    above = moved(south, "lat", 1, False)
    middle = lat_rows // 2
    mid1 = scatter_middle(rows, meta, STEPS, middle, lat_rows, lon_cols)
    meta, below, above = lax.optimization_barrier((meta, below, above))
    to_west, to_east, tall_rates = turn(below, above, strip, rates, lat_rows, lon_cols)
    west = moved(to_east, "lon", -1, True)
    east = moved(to_west, "lon", 1, True)
    mid2 = scatter_middle(rows, meta, middle, lat_rows - STEPS, lat_rows, lon_cols)
    place = lax.axis_index("lat").astype(jnp.int32).reshape(1)
    return diffuse(
        place,
        outer,
        mid1,
        mid2,
        below,
        above,
        west,
        east,
        tall_rates,
        inv_var,
        jacobian,
        lat_rows,
        lon_cols,
        lax.axis_size("lat"),
    )


def solution(mesh):
    in_specs = (
        P(("lon", "lat"), None),
        P(("lon", "lat"), None),
        P(("lon", "lat"), None),
        P(("lon", "lat"), None),
        P(),
        P(),
        P(None, "lat", "lon"),
    )
    out_specs = P(None, "lat", "lon")
    return jax.shard_map(local, mesh=mesh, in_specs=in_specs, out_specs=out_specs, check_vma=False)
```

```python
import functools

import jax
import jax.numpy as jnp
from jax import lax
from jax.experimental import pallas as pl
from jax.experimental.pallas import tpu as pltpu
from jax.sharding import PartitionSpec as P

STEPS = 4
LANES = 128
META = 8
PAD = 8
GROUPS = 8
TILES = 16
MIDDLE_TILES = 32
CHUNKS = 8
UNROLL_RANK = 8
UNROLL_SWEEP = 6
SWEEP_PARTS = 2
OUT_PARTS = 4
F32 = jnp.float32
BF16 = jnp.bfloat16
MIB = 1024 * 1024


def iota(shape, dim):
    return lax.broadcasted_iota(jnp.int32, shape, dim)


def pack_kernel(
    cap,
    owner_hbm,
    cells_hbm,
    weights_hbm,
    rows_hbm,
    out_hbm,
    owner_ref,
    cells_ref,
    weights_ref,
    rows_ref,
    out_ref,
    xd,
    xm,
    yd,
    ym,
    slots_v,
    slots_s,
    in_sems,
    slot_sems,
    out_sems,
):
    groups = owner_ref.shape[0]
    slots = yd.shape[0]
    loads = [
        pltpu.make_async_copy(src, dst, in_sems.at[n])
        for n, (src, dst) in enumerate(
            ((owner_hbm, owner_ref), (cells_hbm, cells_ref), (weights_hbm, weights_ref), (rows_hbm, rows_ref))
        )
    ]
    for load in loads:
        load.start()

    def clear(g, _):
        at = pl.ds(pl.multiple_of(g * LANES, LANES), LANES)
        yd[at, :] = jnp.zeros((LANES, LANES), F32)
        ym[at, :] = jnp.zeros((LANES, LANES), F32)
        return 0

    lax.fori_loop(0, slots // LANES, clear, 0, unroll=2)
    owner_id = iota((LANES, LANES), 0)
    before = (iota((LANES, 2 * LANES), 0) < iota((LANES, 2 * LANES), 1)).astype(F32).astype(BF16)
    for load in loads:
        load.wait()

    def rank_and_stage(g, base):
        own = owner_ref[pl.ds(g, 1), :]
        hit = (own == owner_id).astype(F32)
        seen = jnp.dot(hit.astype(BF16), before, preferred_element_type=F32)
        rank = jnp.sum(hit * (seen[:, :LANES] + base), axis=0, keepdims=True)
        slots_v[pl.ds(g, 1), :] = own * cap + rank.astype(jnp.int32)

        at = pl.ds(pl.multiple_of(g * LANES, LANES), LANES)
        xd[at, :] = rows_ref[at, :].astype(F32)
        cells = cells_ref[:, at]
        weights = weights_ref[:, at]
        c = [cells[k : k + 1] for k in range(4)]
        w = [weights[k : k + 1] for k in range(4)]
        merged = []
        for k in range(4):
            total = w[k]
            for m in range(k + 1, 4):
                total = total + jnp.where(c[m] == c[k], w[m], 0.0)
            for m in range(k):
                total = jnp.where(c[m] == c[k], 0.0, total)
            merged.append(total)
        row = (cells >> 7).astype(F32)
        col = (cells & 127).astype(F32)
        block = jnp.concatenate([row, col] + merged + [jnp.zeros((LANES - 12, LANES), F32)], axis=0)
        xm[at, :] = block.T
        return base + seen[:, LANES:]

    def move(g, _):
        first = pl.multiple_of(g * LANES, LANES)
        for u in range(LANES):
            s = slots_s[g, u]
            yd[pl.ds(s, 1), :] = xd[pl.ds(first + u, 1), :]
            ym[pl.ds(s, 1), :] = xm[pl.ds(first + u, 1), :]
        return 0

    half = groups // 2
    base = jnp.zeros((LANES, LANES), F32)
    copies = []
    for h in range(2):
        base = lax.fori_loop(h * half, (h + 1) * half, rank_and_stage, base, unroll=UNROLL_RANK)
        part = pl.ds(h * half, half)
        copies.append(pltpu.make_async_copy(slots_v.at[part], slots_s.at[part], slot_sems.at[h]))
        copies[h].start()
    for h in range(2):
        copies[h].wait()
        lax.fori_loop(h * half, (h + 1) * half, move, 0)

    pick = (iota((16, LANES), 0) == iota((16, LANES), 1)).astype(F32).astype(BF16)
    left = iota((META, LANES), 1) < cap
    step = 2 * (cap + META)
    batch = slots // LANES // CHUNKS
    stores = []
    for c in range(CHUNKS):
        first_slot = c * batch * LANES
        wide = ym[pl.ds(first_slot, batch * LANES), :].astype(BF16)
        metas = lax.dot_general(pick, wide, (((1,), (1,)), ((), ())), preferred_element_type=F32)
        for u in range(batch):
            data = yd[pl.ds(first_slot + u * LANES, LANES), :]
            low = metas[:META, u * LANES : (u + 1) * LANES]
            high = metas[META:, u * LANES : (u + 1) * LANES]
            first = jnp.where(left, low, pltpu.roll(high, cap, 1))
            second = jnp.where(left, pltpu.roll(low, cap, 1), high)
            block = jnp.concatenate([data[:cap], first, data[cap:], second], axis=0)
            out_ref[pl.ds((c * batch + u) * step, step), :] = block.astype(BF16)
        part = pl.ds(c * batch * step, batch * step)
        stores.append(pltpu.make_async_copy(out_ref.at[part], out_hbm.at[part], out_sems.at[c]))
        stores[c].start()
    for store in stores:
        store.wait()


def pack(owner, cells, weights, rows, devices, cap):
    count = rows.shape[0]
    slots = devices * cap
    groups = count // LANES
    sent = devices * (cap + META)
    hbm = pl.BlockSpec(memory_space=pltpu.HBM)
    return pl.pallas_call(
        functools.partial(pack_kernel, cap),
        out_shape=jax.ShapeDtypeStruct((sent, LANES), BF16),
        in_specs=[hbm] * 4,
        out_specs=hbm,
        scratch_shapes=[
            pltpu.VMEM((groups, LANES), jnp.int32),
            pltpu.VMEM((4, count), jnp.int32),
            pltpu.VMEM((4, count), F32),
            pltpu.VMEM((count, LANES), BF16),
            pltpu.VMEM((sent, LANES), BF16),
            pltpu.VMEM((count, LANES), F32),
            pltpu.VMEM((count, LANES), F32),
            pltpu.VMEM((slots, LANES), F32),
            pltpu.VMEM((slots, LANES), F32),
            pltpu.VMEM((groups, LANES), jnp.int32),
            pltpu.SMEM((groups, LANES), jnp.int32),
            pltpu.SemaphoreType.DMA((4,)),
            pltpu.SemaphoreType.DMA((2,)),
            pltpu.SemaphoreType.DMA((CHUNKS,)),
        ],
        compiler_params=pltpu.CompilerParams(vmem_limit_bytes=60 * MIB),
        cost_estimate=pl.CostEstimate(flops=4_000_000_000, bytes_accessed=40_000_000, transcendentals=0),
        name="pack",
    )(owner.reshape(groups, LANES), cells.T, weights.T, rows)


def column_of(lon_cols, dim_rows):
    p = iota(dim_rows, 0)
    return (p % GROUPS) * (lon_cols // GROUPS) + p // GROUPS


def column_hots(both, lon_cols):
    depth = both.shape[1]
    col_id = column_of(lon_cols, (lon_cols, depth)).astype(F32).astype(BF16)
    col = []
    for k in range(4):
        apart = jnp.broadcast_to(both[4 + k : 5 + k], (16, depth)).astype(BF16)
        apart = jnp.concatenate([apart] * (lon_cols // 16), axis=0) - col_id
        col.append(jnp.maximum(1.0 - apart * apart, 0.0).astype(BF16))
    return col


def row_weights(both, first, count):
    row_id = (iota((count, both.shape[1]), 0) + first).astype(F32)
    return [jnp.where(both[k : k + 1] == row_id, both[8 + k : 9 + k], 0.0) for k in range(4)]


def spread_rows(col, row, which, lon_cols):
    parts = []
    for i in which:
        total = None
        for k in range(4):
            term = jnp.broadcast_to(row[k][i : i + 1], (lon_cols, row[k].shape[1])).astype(BF16) * col[k]
            total = term if total is None else total + term
        parts.append(total)
    return jnp.concatenate(parts, axis=0)


def edge_kernel(
    cap, lat_rows, lon_cols, recv_ref, rates_ref, rows, meta, hots_ref, field_ref, south_ref, north_ref, strip_ref, acc, tmp
):
    slots = rows.shape[0]
    left = iota((META, LANES), 1) < cap
    step = 2 * (cap + META)

    def unpack(b, _):
        block = recv_ref[pl.ds(pl.multiple_of(b * step, 16), step), :].astype(F32)
        data = jnp.concatenate([block[:cap], block[cap + META : 2 * cap + META]], axis=0)
        rows[pl.ds(pl.multiple_of(b * LANES, LANES), LANES), :] = data.astype(BF16)
        first, second = block[cap : cap + META], block[2 * cap + META :]
        meta[b] = jnp.concatenate(
            [
                jnp.where(left, first, pltpu.roll(second, cap, 1)),
                jnp.where(left, pltpu.roll(first, cap, 1), second),
            ],
            axis=0,
        )
        return 0

    lax.fori_loop(0, slots // LANES, unpack, 0, unroll=4)
    field_ref[...] = jnp.zeros_like(field_ref)
    acc[...] = jnp.zeros_like(acc)
    depth = TILES * LANES
    outer = list(range(STEPS)) + list(range(lat_rows - STEPS, lat_rows))
    sides = list(range(STEPS)) + list(range(lon_cols - STEPS, lon_cols))

    def accumulate(t, _):
        data = rows[pl.ds(pl.multiple_of(t * depth, depth), depth), :]
        both = jnp.concatenate([meta[TILES * t + h] for h in range(TILES)], axis=1)
        col = column_hots(both, lon_cols)
        row = row_weights(both, 0, lat_rows)
        here = pl.ds(pl.multiple_of(t * depth, depth), depth)
        for k in range(4):
            hots_ref[k * lon_cols : (k + 1) * lon_cols, here] = col[k]
        rowb = [r.astype(BF16) for r in row]
        field_ref[...] += jnp.dot(spread_rows(col, row, outer, lon_cols), data, preferred_element_type=F32)
        parts = []
        for j in sides:
            total = None
            for k in range(4):
                same = jnp.where(both[4 + k : 5 + k] == float(j), 1.0, 0.0)
                term = jnp.broadcast_to(same, (lat_rows, depth)).astype(BF16) * rowb[k]
                total = term if total is None else total + term
            parts.append(total)
        acc[...] += jnp.dot(jnp.concatenate(parts, axis=0), data, preferred_element_type=F32)
        return 0

    lax.fori_loop(0, slots // depth, accumulate, 0)
    wide = STEPS * lon_cols
    strip_ref[...] = acc[...].astype(BF16)
    tmp[...] = jnp.zeros_like(tmp)
    for ref, first, at in ((south_ref, 0, 0), (north_ref, wide, lat_rows - STEPS)):
        tmp[0:STEPS, :] = rates_ref[at : at + STEPS, :]
        tmp[STEPS : 2 * STEPS, :] = rates_ref[lat_rows + at : lat_rows + at + STEPS, :]
        ref[:wide, :] = field_ref[first : first + wide, :].astype(BF16)
        ref[wide:, :] = tmp[...].astype(BF16)


def scatter_edges(recv, rates, devices, cap, lat_rows, lon_cols):
    slots = devices * cap
    full = pl.BlockSpec(memory_space=pltpu.VMEM)
    wide = STEPS * lon_cols
    shapes = [
        jax.ShapeDtypeStruct((slots, LANES), BF16),
        jax.ShapeDtypeStruct((slots // LANES, 16, LANES), F32),
        jax.ShapeDtypeStruct((4 * lon_cols, slots), BF16),
        jax.ShapeDtypeStruct((2 * wide, LANES), F32),
        jax.ShapeDtypeStruct((wide + 16, LANES), BF16),
        jax.ShapeDtypeStruct((wide + 16, LANES), BF16),
        jax.ShapeDtypeStruct((2 * STEPS * lat_rows, LANES), BF16),
    ]
    return pl.pallas_call(
        functools.partial(edge_kernel, cap, lat_rows, lon_cols),
        out_shape=shapes,
        in_specs=[full] * 2,
        out_specs=[full] * len(shapes),
        scratch_shapes=[pltpu.VMEM((2 * STEPS * lat_rows, LANES), F32), pltpu.VMEM((16, LANES), F32)],
        compiler_params=pltpu.CompilerParams(vmem_limit_bytes=24 * MIB),
        cost_estimate=pl.CostEstimate(flops=5_000_000_000, bytes_accessed=20_000_000, transcendentals=0),
        name="scatter_edges",
    )(recv, rates)


def middle_kernel(first, last, lon_cols, rows_ref, meta_ref, hots_ref, field_ref):
    field_ref[...] = jnp.zeros_like(field_ref)
    depth = MIDDLE_TILES * LANES
    per = 4

    def accumulate(t, _):
        data = rows_ref[pl.ds(pl.multiple_of(t * depth, depth), depth), :]
        both = jnp.concatenate([meta_ref[MIDDLE_TILES * t + h] for h in range(MIDDLE_TILES)], axis=1)
        here = pl.ds(pl.multiple_of(t * depth, depth), depth)
        col = [hots_ref[k * lon_cols : (k + 1) * lon_cols, here] for k in range(4)]
        row = row_weights(both, first, 16)
        for i in range(first, last, per):
            spread = spread_rows(col, row, range(i - first, i - first + per), lon_cols)
            at = pl.ds((i - first) * lon_cols, per * lon_cols)
            field_ref[at, :] += jnp.dot(spread, data, preferred_element_type=F32)
        return 0

    lax.fori_loop(0, rows_ref.shape[0] // depth, accumulate, 0)


def scatter_middle(rows, meta, hots, first, last, lon_cols):
    full = pl.BlockSpec(memory_space=pltpu.VMEM)
    return pl.pallas_call(
        functools.partial(middle_kernel, first, last, lon_cols),
        out_shape=jax.ShapeDtypeStruct(((last - first) * lon_cols, LANES), F32),
        in_specs=[full] * 3,
        out_specs=full,
        compiler_params=pltpu.CompilerParams(vmem_limit_bytes=20 * MIB),
        cost_estimate=pl.CostEstimate(flops=7_000_000_000, bytes_accessed=20_000_000, transcendentals=0),
        name="scatter_middle",
    )(rows, meta, hots)


def turn_kernel(lat_rows, lon_cols, below_ref, above_ref, strip_ref, rates_ref, west_ref, east_ref, tall_ref, cols, wide_rows):
    tall = lat_rows + 2 * STEPS
    wide = STEPS * lon_cols
    below = below_ref[...].astype(F32)
    above = above_ref[...].astype(F32)
    strip = strip_ref[...].astype(F32)
    wide_rows[0] = below
    wide_rows[1] = above
    for c in range(2):
        at = c * tall
        tall_ref[at : at + STEPS, :] = below[wide + c * STEPS : wide + (c + 1) * STEPS]
        tall_ref[at + STEPS : at + STEPS + lat_rows, :] = rates_ref[c * lat_rows : (c + 1) * lat_rows, :]
        tall_ref[at + STEPS + lat_rows : at + tall, :] = above[wide + c * STEPS : wide + (c + 1) * STEPS]
    for side, ref in ((0, west_ref), (1, east_ref)):
        first = side * (lon_cols // GROUPS - STEPS) * GROUPS + side * (GROUPS - 1)
        for j in range(STEPS):
            n = (side * STEPS + j) * lat_rows
            cols[pl.ds(STEPS * STEPS + j, lat_rows, stride=STEPS), :] = strip[n : n + lat_rows]
        for i in range(STEPS):
            picked = pl.ds(i * lon_cols + first, STEPS, stride=GROUPS)
            cols[pl.ds(STEPS * i, STEPS), :] = wide_rows[0, picked, :]
            cols[pl.ds(STEPS * (STEPS + lat_rows + i), STEPS), :] = wide_rows[1, picked, :]
        ref[: STEPS * tall, :] = cols[...].astype(BF16)
        ref[STEPS * tall :, :] = tall_ref[...].astype(BF16)


def turn(below, above, strip, rates, lat_rows, lon_cols):
    full = pl.BlockSpec(memory_space=pltpu.VMEM)
    tall = lat_rows + 2 * STEPS
    side = jax.ShapeDtypeStruct(((STEPS + 2) * tall, LANES), BF16)
    return pl.pallas_call(
        functools.partial(turn_kernel, lat_rows, lon_cols),
        out_shape=[side, side, jax.ShapeDtypeStruct((2 * tall, LANES), F32)],
        in_specs=[full] * 4,
        out_specs=[full] * 3,
        scratch_shapes=[pltpu.VMEM((STEPS * tall, LANES), F32), pltpu.VMEM((2, STEPS * lon_cols + 16, LANES), F32)],
        compiler_params=pltpu.CompilerParams(vmem_limit_bytes=3 * MIB),
        cost_estimate=pl.CostEstimate(flops=1_000_000, bytes_accessed=1_000_000, transcendentals=0),
        name="turn",
    )(below, above, strip, rates)


def diffuse_kernel(
    lat_rows,
    lon_cols,
    lat_devices,
    place_ref,
    outer_ref,
    mid1_ref,
    mid2_ref,
    below_ref,
    above_ref,
    west_ref,
    east_ref,
    rates_ref,
    gain_ref,
    jac_ref,
    out_hbm,
    out_ref,
    ping,
    pong,
    face_x,
    face_y,
    kappa,
    out_sems,
):
    width = lon_cols + 2 * PAD
    tall = lat_rows + 2 * STEPS
    lead = PAD - STEPS
    trail = PAD + lon_cols
    half = (lat_rows - 2 * STEPS) // 2
    part = lon_cols // GROUPS
    span = (part + 2 * STEPS) * GROUPS
    west = west_ref[...].astype(F32)
    east = east_ref[...].astype(F32)

    rest = jnp.zeros((LANES - tall, LANES), F32)
    for c in range(2):
        at = STEPS * tall + c * tall
        kappa[c, 0:lead, :] = jnp.zeros((lead, LANES), F32)
        kappa[c, lead:PAD, :] = jnp.concatenate([west[at : at + tall], rest], axis=0).T[LANES - STEPS :]
        kappa[c, PAD:trail, :] = jnp.concatenate([rates_ref[c * tall : (c + 1) * tall, :], rest], axis=0).T
        kappa[c, trail : trail + STEPS, :] = jnp.concatenate([east[at : at + tall], rest], axis=0).T[:STEPS]
        kappa[c, trail + STEPS :, :] = jnp.zeros((lead, LANES), F32)

    def strips(c):
        return jnp.concatenate(
            [kappa[c, pl.ds(lead + m, GROUPS, stride=part), :] for m in range(part + 2 * STEPS)], axis=0
        )

    kx, ky = strips(0), strips(1)
    ex = 0.5 * (kx + jnp.concatenate([kx[GROUPS:], kx[:GROUPS]], axis=0))
    row = place_ref[0] * lat_rows - STEPS + iota((span, LANES), 1)
    inside = (row >= 0) & (row < lat_rows * lat_devices - 1)
    ny = jnp.where(inside, 0.5 * (ky + pltpu.roll(ky, LANES - 1, 1)), 0.0)
    for i in range(tall):
        at = pl.ds(i * span, span)
        face_x[at, :] = jnp.broadcast_to(ex[:, i : i + 1], (span, LANES))
        face_y[at, :] = jnp.broadcast_to(ny[:, i : i + 1], (span, LANES))

    strip_id = iota((GROUPS, LANES), 0)
    inner = STEPS * GROUPS
    for i in range(tall):
        n = i - STEPS
        if n < 0:
            middle = below_ref[pl.ds(i * lon_cols, lon_cols), :].astype(F32)
        elif n < STEPS:
            middle = outer_ref[pl.ds(n * lon_cols, lon_cols), :]
        elif n < STEPS + half:
            middle = mid1_ref[pl.ds((n - STEPS) * lon_cols, lon_cols), :]
        elif n < STEPS + 2 * half:
            middle = mid2_ref[pl.ds((n - STEPS - half) * lon_cols, lon_cols), :]
        elif n < lat_rows:
            middle = outer_ref[pl.ds((n - 2 * half) * lon_cols, lon_cols), :]
        else:
            middle = above_ref[pl.ds((n - lat_rows) * lon_cols, lon_cols), :].astype(F32)
        ping[pl.ds(i * span + inner, lon_cols), :] = middle
        for q in range(STEPS):
            tail = middle[(part - STEPS + q) * GROUPS : (part - STEPS + q + 1) * GROUPS]
            side = jnp.broadcast_to(west[STEPS * i + q : STEPS * i + q + 1], (GROUPS, LANES))
            before = jnp.where(strip_id == 0, side, pltpu.roll(tail, 1, 0))
            ping[pl.ds(i * span + q * GROUPS, GROUPS), :] = before
            head = middle[q * GROUPS : (q + 1) * GROUPS]
            side = jnp.broadcast_to(east[STEPS * i + q : STEPS * i + q + 1], (GROUPS, LANES))
            after = jnp.where(strip_id == GROUPS - 1, side, pltpu.roll(head, GROUPS - 1, 0))
            ping[pl.ds(i * span + inner + lon_cols + q * GROUPS, GROUPS), :] = after

    for sweep in range(STEPS):
        old, new = (ping, pong) if sweep % 2 == 0 else (pong, ping)
        low, high = sweep + 1, tall - sweep - 1
        first, stop = sweep + 1, span // GROUPS - 1 - sweep
        cuts = [first + (stop - first) * n // SWEEP_PARTS for n in range(SWEEP_PARTS + 1)]
        for at, end in zip(cuts[:-1], cuts[1:]):
            inside_rows = (end - at) * GROUPS

            def load(ref, i, start, count):
                return ref[pl.ds(pl.multiple_of(i * span + start * GROUPS, 8), count), :]

            def one_row(i, carry, old=old, new=new, at=at, count=inside_rows):
                here, flux_below = carry
                above = load(old, i + 1, at - 1, count + 2 * GROUPS)
                flux_y = load(face_y, i, at, count) * (above - here)[GROUPS : count + GROUPS]
                flux_x = load(face_x, i, at - 1, count + GROUPS) * (here[GROUPS:] - here[: count + GROUPS])
                change = flux_x[GROUPS:] - flux_x[:count] + (flux_y - flux_below)
                new[pl.ds(pl.multiple_of(i * span + at * GROUPS, 8), count), :] = here[GROUPS : count + GROUPS] + change
                return above, flux_y

            here = load(old, low, at - 1, inside_rows + 2 * GROUPS)
            start = load(old, low - 1, at, inside_rows)
            start = load(face_y, low - 1, at, inside_rows) * (here[GROUPS : inside_rows + GROUPS] - start)
            lax.fori_loop(low, high, one_row, (here, start), unroll=UNROLL_SWEEP)

    last = ping if STEPS % 2 == 0 else pong
    gain = gain_ref[...]
    jac = jnp.concatenate([jac_ref[...], jac_ref[...]], axis=1)
    levels = jac_ref.shape[0]

    shape = out_hbm.shape
    stores = []
    band = lat_rows // OUT_PARTS
    for h in range(lat_rows // 2):
        pair = []
        for u in range(2):
            at = (2 * h + u + STEPS) * span + inner
            value = jnp.concatenate([last[pl.ds(at + t, part, stride=GROUPS), :] for t in range(GROUPS)], axis=0)
            value = value * gain
            head = value.astype(BF16)
            low = (value - head.astype(F32)).astype(BF16)
            pair.append(jnp.concatenate([head, low], axis=1))
        both = jnp.concatenate(pair, axis=0)
        result = lax.dot_general(jac, both, (((1,), (1,)), ((), ())), preferred_element_type=F32)
        out_ref[pl.ds(2 * h, levels, stride=lat_rows), :] = result[:, :lon_cols]
        out_ref[pl.ds(2 * h + 1, levels, stride=lat_rows), :] = result[:, lon_cols:]
        if (2 * h + 2) % band == 0:
            rows = pl.ds(2 * h + 2 - band, band)
            n = len(stores)
            stores.append(
                pltpu.make_async_copy(out_ref.reshape(shape).at[:, rows, :], out_hbm.at[:, rows, :], out_sems.at[n])
            )
            stores[n].start()
    for store in stores:
        store.wait()


def diffuse(place, outer, mid1, mid2, below, above, west, east, rates, inv_var, jacobian, lat_rows, lon_cols, lats):
    full = pl.BlockSpec(memory_space=pltpu.VMEM)
    levels = jacobian.shape[1]
    tall, width = lat_rows + 2 * STEPS, lon_cols + 2 * PAD
    span = lon_cols + 2 * STEPS * GROUPS
    return pl.pallas_call(
        functools.partial(diffuse_kernel, lat_rows, lon_cols, lats),
        out_shape=jax.ShapeDtypeStruct((levels, lat_rows, lon_cols), F32),
        in_specs=[pl.BlockSpec(memory_space=pltpu.SMEM)] + [full] * 10,
        out_specs=pl.BlockSpec(memory_space=pltpu.HBM),
        scratch_shapes=[pltpu.VMEM((levels * lat_rows, lon_cols), F32)]
        + [pltpu.VMEM((tall * span, LANES), F32)] * 4
        + [pltpu.VMEM((2, width, LANES), F32), pltpu.SemaphoreType.DMA((OUT_PARTS,))],
        compiler_params=pltpu.CompilerParams(vmem_limit_bytes=28 * MIB),
        cost_estimate=pl.CostEstimate(flops=1_000_000_000, bytes_accessed=20_000_000, transcendentals=0),
        name="diffuse",
    )(place, outer, mid1, mid2, below, above, west, east, rates, inv_var.reshape(1, -1), jacobian.T)


def moved(value, axis, step, wrap):
    size = lax.axis_size(axis)
    pairs = [((i + step) % size, i) for i in range(size) if wrap or 0 <= i + step < size]
    return lax.ppermute(value, axis, pairs)


def local(departures, obs_owner, obs_cells, interp_weights, inv_var, jacobian, face_rates):
    devices = lax.axis_size(("lon", "lat"))
    cap = 2 * departures.shape[0] // devices
    lat_rows, lon_cols = face_rates.shape[1:]
    rates = face_rates.reshape(2 * lat_rows, lon_cols)
    send = pack(obs_owner, obs_cells, interp_weights, departures, devices, cap)
    recv = lax.all_to_all(
        send.reshape(devices, cap + META, LANES), ("lon", "lat"), split_axis=0, concat_axis=0, tiled=True
    ).reshape(devices * (cap + META), LANES)
    rows, meta, hots, outer, south, north, strip = scatter_edges(recv, rates, devices, cap, lat_rows, lon_cols)
    below = moved(north, "lat", -1, False)
    above = moved(south, "lat", 1, False)
    middle = lat_rows // 2
    mid1 = scatter_middle(rows, meta, hots, STEPS, middle, lon_cols)
    meta, below, above = lax.optimization_barrier((meta, below, above))
    to_west, to_east, tall_rates = turn(below, above, strip, rates, lat_rows, lon_cols)
    west = moved(to_east, "lon", -1, True)
    east = moved(to_west, "lon", 1, True)
    mid2 = scatter_middle(rows, meta, hots, middle, lat_rows - STEPS, lon_cols)
    place = lax.axis_index("lat").astype(jnp.int32).reshape(1)
    return diffuse(
        place,
        outer,
        mid1,
        mid2,
        below,
        above,
        west,
        east,
        tall_rates,
        inv_var,
        jacobian,
        lat_rows,
        lon_cols,
        lax.axis_size("lat"),
    )


def solution(mesh):
    in_specs = (
        P(("lon", "lat"), None),
        P(("lon", "lat"), None),
        P(("lon", "lat"), None),
        P(("lon", "lat"), None),
        P(),
        P(),
        P(None, "lat", "lon"),
    )
    out_specs = P(None, "lat", "lon")
    return jax.shard_map(local, mesh=mesh, in_specs=in_specs, out_specs=out_specs, check_vma=False)
```

```python
import functools

import jax
import jax.numpy as jnp
from jax import lax
from jax.experimental import pallas as pl
from jax.experimental.pallas import tpu as pltpu
from jax.sharding import PartitionSpec as P

STEPS = 4
LANES = 128
META = 8
PAD = 8
GROUPS = 8
TILES = 16
MIDDLE_TILES = 32
CHUNKS = 8
UNROLL_RANK = 8
UNROLL_SWEEP = 6
SWEEP_PARTS = 2
OUT_PARTS = 4
F32 = jnp.float32
BF16 = jnp.bfloat16
MIB = 1024 * 1024


def iota(shape, dim):
    return lax.broadcasted_iota(jnp.int32, shape, dim)


def pack_kernel(
    cap,
    owner_hbm,
    cells_hbm,
    weights_hbm,
    rows_hbm,
    out_hbm,
    owner_ref,
    cells_ref,
    weights_ref,
    rows_ref,
    out_ref,
    xd,
    xm,
    yd,
    ym,
    slots_v,
    slots_s,
    in_sems,
    slot_sems,
    out_sems,
):
    groups = owner_ref.shape[0]
    slots = yd.shape[0]
    loads = [
        pltpu.make_async_copy(src, dst, in_sems.at[n])
        for n, (src, dst) in enumerate(
            ((owner_hbm, owner_ref), (cells_hbm, cells_ref), (weights_hbm, weights_ref), (rows_hbm, rows_ref))
        )
    ]
    for load in loads:
        load.start()

    def clear(g, _):
        at = pl.ds(pl.multiple_of(g * LANES, LANES), LANES)
        yd[at, :] = jnp.zeros((LANES, LANES), F32)
        ym[at, :] = jnp.zeros((LANES, LANES), F32)
        return 0

    lax.fori_loop(0, slots // LANES, clear, 0, unroll=2)
    owner_id = iota((LANES, LANES), 0)
    before = (iota((LANES, 2 * LANES), 0) < iota((LANES, 2 * LANES), 1)).astype(F32).astype(BF16)
    for load in loads:
        load.wait()

    def rank_and_stage(g, base):
        own = owner_ref[pl.ds(g, 1), :]
        hit = (own == owner_id).astype(F32)
        seen = jnp.dot(hit.astype(BF16), before, preferred_element_type=F32)
        rank = jnp.sum(hit * (seen[:, :LANES] + base), axis=0, keepdims=True)
        slots_v[pl.ds(g, 1), :] = own * cap + rank.astype(jnp.int32)

        at = pl.ds(pl.multiple_of(g * LANES, LANES), LANES)
        xd[at, :] = rows_ref[at, :].astype(F32)
        cells = cells_ref[:, at]
        weights = weights_ref[:, at]
        c = [cells[k : k + 1] for k in range(4)]
        w = [weights[k : k + 1] for k in range(4)]
        merged = []
        for k in range(4):
            total = w[k]
            for m in range(k + 1, 4):
                total = total + jnp.where(c[m] == c[k], w[m], 0.0)
            for m in range(k):
                total = jnp.where(c[m] == c[k], 0.0, total)
            merged.append(total)
        row = (cells >> 7).astype(F32)
        col = (cells & 127).astype(F32)
        block = jnp.concatenate([row, col] + merged + [jnp.zeros((LANES - 12, LANES), F32)], axis=0)
        xm[at, :] = block.T
        return base + seen[:, LANES:]

    def move(g, _):
        first = pl.multiple_of(g * LANES, LANES)
        for u in range(LANES):
            s = slots_s[g, u]
            yd[pl.ds(s, 1), :] = xd[pl.ds(first + u, 1), :]
            ym[pl.ds(s, 1), :] = xm[pl.ds(first + u, 1), :]
        return 0

    half = groups // 2
    base = jnp.zeros((LANES, LANES), F32)
    copies = []
    for h in range(2):
        base = lax.fori_loop(h * half, (h + 1) * half, rank_and_stage, base, unroll=UNROLL_RANK)
        part = pl.ds(h * half, half)
        copies.append(pltpu.make_async_copy(slots_v.at[part], slots_s.at[part], slot_sems.at[h]))
        copies[h].start()
    for h in range(2):
        copies[h].wait()
        lax.fori_loop(h * half, (h + 1) * half, move, 0)

    pick = (iota((16, LANES), 0) == iota((16, LANES), 1)).astype(F32).astype(BF16)
    left = iota((META, LANES), 1) < cap
    step = 2 * (cap + META)
    batch = slots // LANES // CHUNKS
    stores = []
    for c in range(CHUNKS):
        first_slot = c * batch * LANES
        wide = ym[pl.ds(first_slot, batch * LANES), :].astype(BF16)
        metas = lax.dot_general(pick, wide, (((1,), (1,)), ((), ())), preferred_element_type=F32)
        for u in range(batch):
            data = yd[pl.ds(first_slot + u * LANES, LANES), :]
            low = metas[:META, u * LANES : (u + 1) * LANES]
            high = metas[META:, u * LANES : (u + 1) * LANES]
            first = jnp.where(left, low, pltpu.roll(high, cap, 1))
            second = jnp.where(left, pltpu.roll(low, cap, 1), high)
            block = jnp.concatenate([data[:cap], first, data[cap:], second], axis=0)
            out_ref[pl.ds((c * batch + u) * step, step), :] = block.astype(BF16)
        part = pl.ds(c * batch * step, batch * step)
        stores.append(pltpu.make_async_copy(out_ref.at[part], out_hbm.at[part], out_sems.at[c]))
        stores[c].start()
    for store in stores:
        store.wait()


def pack(owner, cells, weights, rows, devices, cap):
    count = rows.shape[0]
    slots = devices * cap
    groups = count // LANES
    sent = devices * (cap + META)
    hbm = pl.BlockSpec(memory_space=pltpu.HBM)
    return pl.pallas_call(
        functools.partial(pack_kernel, cap),
        out_shape=jax.ShapeDtypeStruct((sent, LANES), BF16),
        in_specs=[hbm] * 4,
        out_specs=hbm,
        scratch_shapes=[
            pltpu.VMEM((groups, LANES), jnp.int32),
            pltpu.VMEM((4, count), jnp.int32),
            pltpu.VMEM((4, count), F32),
            pltpu.VMEM((count, LANES), BF16),
            pltpu.VMEM((sent, LANES), BF16),
            pltpu.VMEM((count, LANES), F32),
            pltpu.VMEM((count, LANES), F32),
            pltpu.VMEM((slots, LANES), F32),
            pltpu.VMEM((slots, LANES), F32),
            pltpu.VMEM((groups, LANES), jnp.int32),
            pltpu.SMEM((groups, LANES), jnp.int32),
            pltpu.SemaphoreType.DMA((4,)),
            pltpu.SemaphoreType.DMA((2,)),
            pltpu.SemaphoreType.DMA((CHUNKS,)),
        ],
        compiler_params=pltpu.CompilerParams(vmem_limit_bytes=60 * MIB),
        cost_estimate=pl.CostEstimate(flops=4_000_000_000, bytes_accessed=40_000_000, transcendentals=0),
        name="pack",
    )(owner.reshape(groups, LANES), cells.T, weights.T, rows)


def column_of(lon_cols, dim_rows):
    p = iota(dim_rows, 0)
    return (p % GROUPS) * (lon_cols // GROUPS) + p // GROUPS


def column_hots(both, lon_cols):
    depth = both.shape[1]
    col_id = column_of(lon_cols, (lon_cols, depth)).astype(F32).astype(BF16)
    col = []
    for k in range(4):
        apart = jnp.broadcast_to(both[4 + k : 5 + k], (16, depth)).astype(BF16)
        apart = jnp.concatenate([apart] * (lon_cols // 16), axis=0) - col_id
        col.append(jnp.maximum(1.0 - apart * apart, 0.0).astype(BF16))
    return col


def row_weights(both, first, count):
    row_id = (iota((count, both.shape[1]), 0) + first).astype(F32)
    return [jnp.where(both[k : k + 1] == row_id, both[8 + k : 9 + k], 0.0) for k in range(4)]


def spread_rows(col, row, which, lon_cols):
    parts = []
    for i in which:
        total = None
        for k in range(4):
            term = jnp.broadcast_to(row[k][i : i + 1], (lon_cols, row[k].shape[1])).astype(BF16) * col[k]
            total = term if total is None else total + term
        parts.append(total)
    return jnp.concatenate(parts, axis=0)


def edge_kernel(
    cap, lat_rows, lon_cols, recv_ref, rates_ref, rows, meta, hots_ref, field_ref, south_ref, north_ref, strip_ref, acc, tmp
):
    slots = rows.shape[0]
    left = iota((META, LANES), 1) < cap
    step = 2 * (cap + META)

    def unpack(b, _):
        block = recv_ref[pl.ds(pl.multiple_of(b * step, 16), step), :].astype(F32)
        data = jnp.concatenate([block[:cap], block[cap + META : 2 * cap + META]], axis=0)
        rows[pl.ds(pl.multiple_of(b * LANES, LANES), LANES), :] = data.astype(BF16)
        first, second = block[cap : cap + META], block[2 * cap + META :]
        meta[b] = jnp.concatenate(
            [
                jnp.where(left, first, pltpu.roll(second, cap, 1)),
                jnp.where(left, pltpu.roll(first, cap, 1), second),
            ],
            axis=0,
        )
        return 0

    lax.fori_loop(0, slots // LANES, unpack, 0, unroll=16)
    field_ref[...] = jnp.zeros_like(field_ref)
    acc[...] = jnp.zeros_like(acc)
    depth = TILES * LANES
    outer = list(range(STEPS)) + list(range(lat_rows - STEPS, lat_rows))
    sides = list(range(STEPS)) + list(range(lon_cols - STEPS, lon_cols))

    def accumulate(t, _):
        data = rows[pl.ds(pl.multiple_of(t * depth, depth), depth), :]
        both = jnp.concatenate([meta[TILES * t + h] for h in range(TILES)], axis=1)
        col = column_hots(both, lon_cols)
        row = row_weights(both, 0, lat_rows)
        here = pl.ds(pl.multiple_of(t * depth, depth), depth)
        for k in range(4):
            hots_ref[k * lon_cols : (k + 1) * lon_cols, here] = col[k]
        rowb = [r.astype(BF16) for r in row]
        field_ref[...] += jnp.dot(spread_rows(col, row, outer, lon_cols), data, preferred_element_type=F32)
        parts = []
        for j in sides:
            total = None
            for k in range(4):
                same = jnp.where(both[4 + k : 5 + k] == float(j), 1.0, 0.0)
                term = jnp.broadcast_to(same, (lat_rows, depth)).astype(BF16) * rowb[k]
                total = term if total is None else total + term
            parts.append(total)
        acc[...] += jnp.dot(jnp.concatenate(parts, axis=0), data, preferred_element_type=F32)
        return 0

    lax.fori_loop(0, slots // depth, accumulate, 0)
    wide = STEPS * lon_cols
    strip_ref[...] = acc[...].astype(BF16)
    tmp[...] = jnp.zeros_like(tmp)
    for ref, first, at in ((south_ref, 0, 0), (north_ref, wide, lat_rows - STEPS)):
        tmp[0:STEPS, :] = rates_ref[at : at + STEPS, :]
        tmp[STEPS : 2 * STEPS, :] = rates_ref[lat_rows + at : lat_rows + at + STEPS, :]
        ref[:wide, :] = field_ref[first : first + wide, :].astype(BF16)
        ref[wide:, :] = tmp[...].astype(BF16)


def scatter_edges(recv, rates, devices, cap, lat_rows, lon_cols):
    slots = devices * cap
    full = pl.BlockSpec(memory_space=pltpu.VMEM)
    wide = STEPS * lon_cols
    shapes = [
        jax.ShapeDtypeStruct((slots, LANES), BF16),
        jax.ShapeDtypeStruct((slots // LANES, 16, LANES), F32),
        jax.ShapeDtypeStruct((4 * lon_cols, slots), BF16),
        jax.ShapeDtypeStruct((2 * wide, LANES), F32),
        jax.ShapeDtypeStruct((wide + 16, LANES), BF16),
        jax.ShapeDtypeStruct((wide + 16, LANES), BF16),
        jax.ShapeDtypeStruct((2 * STEPS * lat_rows, LANES), BF16),
    ]
    return pl.pallas_call(
        functools.partial(edge_kernel, cap, lat_rows, lon_cols),
        out_shape=shapes,
        in_specs=[full] * 2,
        out_specs=[full] * len(shapes),
        scratch_shapes=[pltpu.VMEM((2 * STEPS * lat_rows, LANES), F32), pltpu.VMEM((16, LANES), F32)],
        compiler_params=pltpu.CompilerParams(vmem_limit_bytes=24 * MIB),
        cost_estimate=pl.CostEstimate(flops=5_000_000_000, bytes_accessed=20_000_000, transcendentals=0),
        name="scatter_edges",
    )(recv, rates)


def middle_kernel(first, last, lon_cols, rows_ref, meta_ref, hots_ref, field_ref):
    field_ref[...] = jnp.zeros_like(field_ref)
    depth = MIDDLE_TILES * LANES
    per = 4

    def accumulate(t, _):
        data = rows_ref[pl.ds(pl.multiple_of(t * depth, depth), depth), :]
        both = jnp.concatenate([meta_ref[MIDDLE_TILES * t + h] for h in range(MIDDLE_TILES)], axis=1)
        here = pl.ds(pl.multiple_of(t * depth, depth), depth)
        col = [hots_ref[k * lon_cols : (k + 1) * lon_cols, here] for k in range(4)]
        row = row_weights(both, first, 16)
        for i in range(first, last, per):
            spread = spread_rows(col, row, range(i - first, i - first + per), lon_cols)
            at = pl.ds((i - first) * lon_cols, per * lon_cols)
            field_ref[at, :] += jnp.dot(spread, data, preferred_element_type=F32)
        return 0

    lax.fori_loop(0, rows_ref.shape[0] // depth, accumulate, 0)


def scatter_middle(rows, meta, hots, first, last, lon_cols):
    full = pl.BlockSpec(memory_space=pltpu.VMEM)
    return pl.pallas_call(
        functools.partial(middle_kernel, first, last, lon_cols),
        out_shape=jax.ShapeDtypeStruct(((last - first) * lon_cols, LANES), F32),
        in_specs=[full] * 3,
        out_specs=full,
        compiler_params=pltpu.CompilerParams(vmem_limit_bytes=20 * MIB),
        cost_estimate=pl.CostEstimate(flops=7_000_000_000, bytes_accessed=20_000_000, transcendentals=0),
        name="scatter_middle",
    )(rows, meta, hots)


def turn_kernel(lat_rows, lon_cols, below_ref, above_ref, strip_ref, rates_ref, west_ref, east_ref, tall_ref, cols, wide_rows):
    tall = lat_rows + 2 * STEPS
    wide = STEPS * lon_cols
    below = below_ref[...].astype(F32)
    above = above_ref[...].astype(F32)
    strip = strip_ref[...].astype(F32)
    wide_rows[0] = below
    wide_rows[1] = above
    for c in range(2):
        at = c * tall
        tall_ref[at : at + STEPS, :] = below[wide + c * STEPS : wide + (c + 1) * STEPS]
        tall_ref[at + STEPS : at + STEPS + lat_rows, :] = rates_ref[c * lat_rows : (c + 1) * lat_rows, :]
        tall_ref[at + STEPS + lat_rows : at + tall, :] = above[wide + c * STEPS : wide + (c + 1) * STEPS]
    for side, ref in ((0, west_ref), (1, east_ref)):
        first = side * (lon_cols // GROUPS - STEPS) * GROUPS + side * (GROUPS - 1)
        for j in range(STEPS):
            n = (side * STEPS + j) * lat_rows
            cols[pl.ds(STEPS * STEPS + j, lat_rows, stride=STEPS), :] = strip[n : n + lat_rows]
        for i in range(STEPS):
            picked = pl.ds(i * lon_cols + first, STEPS, stride=GROUPS)
            cols[pl.ds(STEPS * i, STEPS), :] = wide_rows[0, picked, :]
            cols[pl.ds(STEPS * (STEPS + lat_rows + i), STEPS), :] = wide_rows[1, picked, :]
        ref[: STEPS * tall, :] = cols[...].astype(BF16)
        ref[STEPS * tall :, :] = tall_ref[...].astype(BF16)


def turn(below, above, strip, rates, lat_rows, lon_cols):
    full = pl.BlockSpec(memory_space=pltpu.VMEM)
    tall = lat_rows + 2 * STEPS
    side = jax.ShapeDtypeStruct(((STEPS + 2) * tall, LANES), BF16)
    return pl.pallas_call(
        functools.partial(turn_kernel, lat_rows, lon_cols),
        out_shape=[side, side, jax.ShapeDtypeStruct((2 * tall, LANES), F32)],
        in_specs=[full] * 4,
        out_specs=[full] * 3,
        scratch_shapes=[pltpu.VMEM((STEPS * tall, LANES), F32), pltpu.VMEM((2, STEPS * lon_cols + 16, LANES), F32)],
        compiler_params=pltpu.CompilerParams(vmem_limit_bytes=3 * MIB),
        cost_estimate=pl.CostEstimate(flops=1_000_000, bytes_accessed=1_000_000, transcendentals=0),
        name="turn",
    )(below, above, strip, rates)


def diffuse_kernel(
    lat_rows,
    lon_cols,
    lat_devices,
    place_ref,
    outer_ref,
    mid1_ref,
    mid2_ref,
    below_ref,
    above_ref,
    west_ref,
    east_ref,
    rates_ref,
    gain_ref,
    jac_ref,
    out_hbm,
    out_ref,
    ping,
    pong,
    face_x,
    face_y,
    kappa,
    out_sems,
):
    width = lon_cols + 2 * PAD
    tall = lat_rows + 2 * STEPS
    lead = PAD - STEPS
    trail = PAD + lon_cols
    half = (lat_rows - 2 * STEPS) // 2
    part = lon_cols // GROUPS
    span = (part + 2 * STEPS) * GROUPS
    west = west_ref[...].astype(F32)
    east = east_ref[...].astype(F32)

    rest = jnp.zeros((LANES - tall, LANES), F32)
    for c in range(2):
        at = STEPS * tall + c * tall
        kappa[c, 0:lead, :] = jnp.zeros((lead, LANES), F32)
        kappa[c, lead:PAD, :] = jnp.concatenate([west[at : at + tall], rest], axis=0).T[LANES - STEPS :]
        kappa[c, PAD:trail, :] = jnp.concatenate([rates_ref[c * tall : (c + 1) * tall, :], rest], axis=0).T
        kappa[c, trail : trail + STEPS, :] = jnp.concatenate([east[at : at + tall], rest], axis=0).T[:STEPS]
        kappa[c, trail + STEPS :, :] = jnp.zeros((lead, LANES), F32)

    def strips(c):
        return jnp.concatenate(
            [kappa[c, pl.ds(lead + m, GROUPS, stride=part), :] for m in range(part + 2 * STEPS)], axis=0
        )

    kx, ky = strips(0), strips(1)
    ex = 0.5 * (kx + jnp.concatenate([kx[GROUPS:], kx[:GROUPS]], axis=0))
    row = place_ref[0] * lat_rows - STEPS + iota((span, LANES), 1)
    inside = (row >= 0) & (row < lat_rows * lat_devices - 1)
    ny = jnp.where(inside, 0.5 * (ky + pltpu.roll(ky, LANES - 1, 1)), 0.0)
    left = jnp.where(iota((2 * span, LANES), 1) < tall, jnp.concatenate([ex, ny], axis=0), 0.0)
    pieces = None
    for n in range(3):
        piece = left.astype(BF16).astype(F32)
        left = left - piece
        pieces = piece if n == 0 else pieces + pltpu.roll(piece, n * tall, 1)
    pieces = pieces.astype(BF16)
    lane = iota((LANES, LANES), 0) % tall
    for i in range(0, tall, 2):
        choice = jnp.concatenate([(lane == i).astype(F32), (lane == i + 1).astype(F32)], axis=1).astype(BF16)
        spread = jnp.dot(pieces, choice, preferred_element_type=F32)
        for u in range(2):
            at = pl.ds((i + u) * span, span)
            face_x[at, :] = spread[:span, u * LANES : (u + 1) * LANES]
            face_y[at, :] = spread[span:, u * LANES : (u + 1) * LANES]

    strip_id = iota((GROUPS, LANES), 0)
    inner = STEPS * GROUPS
    for i in range(tall):
        n = i - STEPS
        if n < 0:
            middle = below_ref[pl.ds(i * lon_cols, lon_cols), :].astype(F32)
        elif n < STEPS:
            middle = outer_ref[pl.ds(n * lon_cols, lon_cols), :]
        elif n < STEPS + half:
            middle = mid1_ref[pl.ds((n - STEPS) * lon_cols, lon_cols), :]
        elif n < STEPS + 2 * half:
            middle = mid2_ref[pl.ds((n - STEPS - half) * lon_cols, lon_cols), :]
        elif n < lat_rows:
            middle = outer_ref[pl.ds((n - 2 * half) * lon_cols, lon_cols), :]
        else:
            middle = above_ref[pl.ds((n - lat_rows) * lon_cols, lon_cols), :].astype(F32)
        ping[pl.ds(i * span + inner, lon_cols), :] = middle
        for q in range(STEPS):
            tail = middle[(part - STEPS + q) * GROUPS : (part - STEPS + q + 1) * GROUPS]
            side = jnp.broadcast_to(west[STEPS * i + q : STEPS * i + q + 1], (GROUPS, LANES))
            before = jnp.where(strip_id == 0, side, pltpu.roll(tail, 1, 0))
            ping[pl.ds(i * span + q * GROUPS, GROUPS), :] = before
            head = middle[q * GROUPS : (q + 1) * GROUPS]
            side = jnp.broadcast_to(east[STEPS * i + q : STEPS * i + q + 1], (GROUPS, LANES))
            after = jnp.where(strip_id == GROUPS - 1, side, pltpu.roll(head, GROUPS - 1, 0))
            ping[pl.ds(i * span + inner + lon_cols + q * GROUPS, GROUPS), :] = after

    for sweep in range(STEPS):
        old, new = (ping, pong) if sweep % 2 == 0 else (pong, ping)
        low, high = sweep + 1, tall - sweep - 1
        first, stop = sweep + 1, span // GROUPS - 1 - sweep
        cuts = [first + (stop - first) * n // SWEEP_PARTS for n in range(SWEEP_PARTS + 1)]
        for at, end in zip(cuts[:-1], cuts[1:]):
            inside_rows = (end - at) * GROUPS

            def load(ref, i, start, count):
                return ref[pl.ds(pl.multiple_of(i * span + start * GROUPS, 8), count), :]

            def one_row(i, carry, old=old, new=new, at=at, count=inside_rows):
                here, flux_below = carry
                above = load(old, i + 1, at - 1, count + 2 * GROUPS)
                flux_y = load(face_y, i, at, count) * (above - here)[GROUPS : count + GROUPS]
                flux_x = load(face_x, i, at - 1, count + GROUPS) * (here[GROUPS:] - here[: count + GROUPS])
                change = flux_x[GROUPS:] - flux_x[:count] + (flux_y - flux_below)
                new[pl.ds(pl.multiple_of(i * span + at * GROUPS, 8), count), :] = here[GROUPS : count + GROUPS] + change
                return above, flux_y

            here = load(old, low, at - 1, inside_rows + 2 * GROUPS)
            start = load(old, low - 1, at, inside_rows)
            start = load(face_y, low - 1, at, inside_rows) * (here[GROUPS : inside_rows + GROUPS] - start)
            lax.fori_loop(low, high, one_row, (here, start), unroll=UNROLL_SWEEP)

    last = ping if STEPS % 2 == 0 else pong
    gain = gain_ref[...]
    jac = jnp.concatenate([jac_ref[...], jac_ref[...]], axis=1)
    levels = jac_ref.shape[0]

    shape = out_hbm.shape
    stores = []
    band = lat_rows // OUT_PARTS
    for h in range(lat_rows // 2):
        pair = []
        for u in range(2):
            at = (2 * h + u + STEPS) * span + inner
            value = jnp.concatenate([last[pl.ds(at + t, part, stride=GROUPS), :] for t in range(GROUPS)], axis=0)
            value = value * gain
            head = value.astype(BF16)
            low = (value - head.astype(F32)).astype(BF16)
            pair.append(jnp.concatenate([head, low], axis=1))
        both = jnp.concatenate(pair, axis=0)
        result = lax.dot_general(jac, both, (((1,), (1,)), ((), ())), preferred_element_type=F32)
        out_ref[pl.ds(2 * h, levels, stride=lat_rows), :] = result[:, :lon_cols]
        out_ref[pl.ds(2 * h + 1, levels, stride=lat_rows), :] = result[:, lon_cols:]
        if (2 * h + 2) % band == 0:
            rows = pl.ds(2 * h + 2 - band, band)
            n = len(stores)
            stores.append(
                pltpu.make_async_copy(out_ref.reshape(shape).at[:, rows, :], out_hbm.at[:, rows, :], out_sems.at[n])
            )
            stores[n].start()
    for store in stores:
        store.wait()


def diffuse(place, outer, mid1, mid2, below, above, west, east, rates, inv_var, jacobian, lat_rows, lon_cols, lats):
    full = pl.BlockSpec(memory_space=pltpu.VMEM)
    levels = jacobian.shape[1]
    tall, width = lat_rows + 2 * STEPS, lon_cols + 2 * PAD
    span = lon_cols + 2 * STEPS * GROUPS
    return pl.pallas_call(
        functools.partial(diffuse_kernel, lat_rows, lon_cols, lats),
        out_shape=jax.ShapeDtypeStruct((levels, lat_rows, lon_cols), F32),
        in_specs=[pl.BlockSpec(memory_space=pltpu.SMEM)] + [full] * 10,
        out_specs=pl.BlockSpec(memory_space=pltpu.HBM),
        scratch_shapes=[pltpu.VMEM((levels * lat_rows, lon_cols), F32)]
        + [pltpu.VMEM((tall * span, LANES), F32)] * 4
        + [pltpu.VMEM((2, width, LANES), F32), pltpu.SemaphoreType.DMA((OUT_PARTS,))],
        compiler_params=pltpu.CompilerParams(vmem_limit_bytes=28 * MIB),
        cost_estimate=pl.CostEstimate(flops=1_000_000_000, bytes_accessed=20_000_000, transcendentals=0),
        name="diffuse",
    )(place, outer, mid1, mid2, below, above, west, east, rates, inv_var.reshape(1, -1), jacobian.T)


def moved(value, axis, step, wrap):
    size = lax.axis_size(axis)
    pairs = [((i + step) % size, i) for i in range(size) if wrap or 0 <= i + step < size]
    return lax.ppermute(value, axis, pairs)


def local(departures, obs_owner, obs_cells, interp_weights, inv_var, jacobian, face_rates):
    devices = lax.axis_size(("lon", "lat"))
    cap = 2 * departures.shape[0] // devices
    lat_rows, lon_cols = face_rates.shape[1:]
    rates = face_rates.reshape(2 * lat_rows, lon_cols)
    send = pack(obs_owner, obs_cells, interp_weights, departures, devices, cap)
    recv = lax.all_to_all(
        send.reshape(devices, cap + META, LANES), ("lon", "lat"), split_axis=0, concat_axis=0, tiled=True
    ).reshape(devices * (cap + META), LANES)
    rows, meta, hots, outer, south, north, strip = scatter_edges(recv, rates, devices, cap, lat_rows, lon_cols)
    below = moved(north, "lat", -1, False)
    above = moved(south, "lat", 1, False)
    middle = lat_rows // 2
    mid1 = scatter_middle(rows, meta, hots, STEPS, middle, lon_cols)
    meta, below, above = lax.optimization_barrier((meta, below, above))
    to_west, to_east, tall_rates = turn(below, above, strip, rates, lat_rows, lon_cols)
    west = moved(to_east, "lon", -1, True)
    east = moved(to_west, "lon", 1, True)
    mid2 = scatter_middle(rows, meta, hots, middle, lat_rows - STEPS, lon_cols)
    place = lax.axis_index("lat").astype(jnp.int32).reshape(1)
    return diffuse(
        place,
        outer,
        mid1,
        mid2,
        below,
        above,
        west,
        east,
        tall_rates,
        inv_var,
        jacobian,
        lat_rows,
        lon_cols,
        lax.axis_size("lat"),
    )


def solution(mesh):
    in_specs = (
        P(("lon", "lat"), None),
        P(("lon", "lat"), None),
        P(("lon", "lat"), None),
        P(("lon", "lat"), None),
        P(),
        P(),
        P(None, "lat", "lon"),
    )
    out_specs = P(None, "lat", "lon")
    return jax.shard_map(local, mesh=mesh, in_specs=in_specs, out_specs=out_specs, check_vma=False)
```

```python
import functools

import jax
import jax.numpy as jnp
from jax import lax
from jax.experimental import pallas as pl
from jax.experimental.pallas import tpu as pltpu
from jax.sharding import PartitionSpec as P

STEPS = 4
LANES = 128
META = 8
PAD = 8
GROUPS = 8
TILES = 16
MIDDLE_TILES = 32
CHUNKS = 8
UNROLL_RANK = 8
UNROLL_SWEEP = 12
SWEEP_PARTS = 2
OUT_PARTS = 8
F32 = jnp.float32
BF16 = jnp.bfloat16
MIB = 1024 * 1024


def iota(shape, dim):
    return lax.broadcasted_iota(jnp.int32, shape, dim)


def pack_kernel(
    cap,
    owner_hbm,
    cells_hbm,
    weights_hbm,
    rows_hbm,
    out_hbm,
    owner_ref,
    cells_ref,
    weights_ref,
    rows_ref,
    out_ref,
    xd,
    xm,
    yd,
    ym,
    slots_v,
    slots_s,
    in_sems,
    slot_sems,
    out_sems,
):
    groups = owner_ref.shape[0]
    slots = yd.shape[0]
    loads = [
        pltpu.make_async_copy(src, dst, in_sems.at[n])
        for n, (src, dst) in enumerate(
            ((owner_hbm, owner_ref), (cells_hbm, cells_ref), (weights_hbm, weights_ref), (rows_hbm, rows_ref))
        )
    ]
    for load in loads:
        load.start()

    def clear(g, _):
        at = pl.ds(pl.multiple_of(g * LANES, LANES), LANES)
        yd[at, :] = jnp.zeros((LANES, LANES), F32)
        ym[at, :] = jnp.zeros((LANES, LANES), F32)
        return 0

    lax.fori_loop(0, slots // LANES, clear, 0, unroll=2)
    owner_id = iota((LANES, LANES), 0)
    before = (iota((LANES, 2 * LANES), 0) < iota((LANES, 2 * LANES), 1)).astype(F32).astype(BF16)
    for load in loads:
        load.wait()

    def rank_and_stage(g, base):
        own = owner_ref[pl.ds(g, 1), :]
        hit = (own == owner_id).astype(F32)
        seen = jnp.dot(hit.astype(BF16), before, preferred_element_type=F32)
        rank = jnp.sum(hit * (seen[:, :LANES] + base), axis=0, keepdims=True)
        slots_v[pl.ds(g, 1), :] = own * cap + rank.astype(jnp.int32)

        at = pl.ds(pl.multiple_of(g * LANES, LANES), LANES)
        xd[at, :] = rows_ref[at, :].astype(F32)
        cells = cells_ref[:, at]
        weights = weights_ref[:, at]
        c = [cells[k : k + 1] for k in range(4)]
        w = [weights[k : k + 1] for k in range(4)]
        merged = []
        for k in range(4):
            total = w[k]
            for m in range(k + 1, 4):
                total = total + jnp.where(c[m] == c[k], w[m], 0.0)
            for m in range(k):
                total = jnp.where(c[m] == c[k], 0.0, total)
            merged.append(total)
        row = (cells >> 7).astype(F32)
        col = (cells & 127).astype(F32)
        block = jnp.concatenate([row, col] + merged + [jnp.zeros((LANES - 12, LANES), F32)], axis=0)
        xm[at, :] = block.T
        return base + seen[:, LANES:]

    def move(g, _):
        first = pl.multiple_of(g * LANES, LANES)
        for start in range(0, LANES, 4):
            batch = range(start, start + 4)
            where = [slots_s[g, u] for u in batch]
            data = [xd[pl.ds(first + u, 1), :] for u in batch]
            meta = [xm[pl.ds(first + u, 1), :] for u in batch]
            for s, value in zip(where, data):
                yd[pl.ds(s, 1), :] = value
            for s, value in zip(where, meta):
                ym[pl.ds(s, 1), :] = value
        return 0

    half = groups // 2
    base = jnp.zeros((LANES, LANES), F32)
    copies = []
    for h in range(2):
        base = lax.fori_loop(h * half, (h + 1) * half, rank_and_stage, base, unroll=UNROLL_RANK)
        part = pl.ds(h * half, half)
        copies.append(pltpu.make_async_copy(slots_v.at[part], slots_s.at[part], slot_sems.at[h]))
        copies[h].start()
    for h in range(2):
        copies[h].wait()
        lax.fori_loop(h * half, (h + 1) * half, move, 0)

    pick = (iota((16, LANES), 0) == iota((16, LANES), 1)).astype(F32).astype(BF16)
    left = iota((META, LANES), 1) < cap
    step = 2 * (cap + META)
    batch = slots // LANES // CHUNKS
    stores = []
    for c in range(CHUNKS):
        first_slot = c * batch * LANES
        wide = ym[pl.ds(first_slot, batch * LANES), :].astype(BF16)
        metas = lax.dot_general(pick, wide, (((1,), (1,)), ((), ())), preferred_element_type=F32)
        for u in range(batch):
            data = yd[pl.ds(first_slot + u * LANES, LANES), :]
            low = metas[:META, u * LANES : (u + 1) * LANES]
            high = metas[META:, u * LANES : (u + 1) * LANES]
            first = jnp.where(left, low, pltpu.roll(high, cap, 1))
            second = jnp.where(left, pltpu.roll(low, cap, 1), high)
            block = jnp.concatenate([data[:cap], first, data[cap:], second], axis=0)
            out_ref[pl.ds((c * batch + u) * step, step), :] = block.astype(BF16)
        part = pl.ds(c * batch * step, batch * step)
        stores.append(pltpu.make_async_copy(out_ref.at[part], out_hbm.at[part], out_sems.at[c]))
        stores[c].start()
    for store in stores:
        store.wait()


def pack(owner, cells, weights, rows, devices, cap):
    count = rows.shape[0]
    slots = devices * cap
    groups = count // LANES
    sent = devices * (cap + META)
    hbm = pl.BlockSpec(memory_space=pltpu.HBM)
    return pl.pallas_call(
        functools.partial(pack_kernel, cap),
        out_shape=jax.ShapeDtypeStruct((sent, LANES), BF16),
        in_specs=[hbm] * 4,
        out_specs=hbm,
        scratch_shapes=[
            pltpu.VMEM((groups, LANES), jnp.int32),
            pltpu.VMEM((4, count), jnp.int32),
            pltpu.VMEM((4, count), F32),
            pltpu.VMEM((count, LANES), BF16),
            pltpu.VMEM((sent, LANES), BF16),
            pltpu.VMEM((count, LANES), F32),
            pltpu.VMEM((count, LANES), F32),
            pltpu.VMEM((slots, LANES), F32),
            pltpu.VMEM((slots, LANES), F32),
            pltpu.VMEM((groups, LANES), jnp.int32),
            pltpu.SMEM((groups, LANES), jnp.int32),
            pltpu.SemaphoreType.DMA((4,)),
            pltpu.SemaphoreType.DMA((2,)),
            pltpu.SemaphoreType.DMA((CHUNKS,)),
        ],
        compiler_params=pltpu.CompilerParams(vmem_limit_bytes=60 * MIB),
        cost_estimate=pl.CostEstimate(flops=4_000_000_000, bytes_accessed=40_000_000, transcendentals=0),
        name="pack",
    )(owner.reshape(groups, LANES), cells.T, weights.T, rows)


def column_of(lon_cols, dim_rows):
    p = iota(dim_rows, 0)
    return (p % GROUPS) * (lon_cols // GROUPS) + p // GROUPS


def column_hots(both, lon_cols):
    depth = both.shape[1]
    col_id = column_of(lon_cols, (lon_cols, depth)).astype(F32).astype(BF16)
    col = []
    for k in range(4):
        apart = jnp.broadcast_to(both[4 + k : 5 + k], (16, depth)).astype(BF16)
        apart = jnp.concatenate([apart] * (lon_cols // 16), axis=0) - col_id
        col.append(jnp.maximum(1.0 - apart * apart, 0.0).astype(BF16))
    return col


def row_weights(both, first, count):
    row_id = (iota((count, both.shape[1]), 0) + first).astype(F32)
    return [jnp.where(both[k : k + 1] == row_id, both[8 + k : 9 + k], 0.0) for k in range(4)]


def spread_rows(col, row, which, lon_cols):
    parts = []
    for i in which:
        total = None
        for k in range(4):
            term = jnp.broadcast_to(row[k][i : i + 1], (lon_cols, row[k].shape[1])).astype(BF16) * col[k]
            total = term if total is None else total + term
        parts.append(total)
    return jnp.concatenate(parts, axis=0)


def edge_kernel(
    cap, lat_rows, lon_cols, recv_ref, rates_ref, rows, meta, hots_ref, field_ref, south_ref, north_ref, strip_ref, acc, tmp
):
    slots = rows.shape[0]
    left = iota((META, LANES), 1) < cap
    step = 2 * (cap + META)

    def unpack(b, _):
        block = recv_ref[pl.ds(pl.multiple_of(b * step, 16), step), :].astype(F32)
        data = jnp.concatenate([block[:cap], block[cap + META : 2 * cap + META]], axis=0)
        rows[pl.ds(pl.multiple_of(b * LANES, LANES), LANES), :] = data.astype(BF16)
        first, second = block[cap : cap + META], block[2 * cap + META :]
        meta[b] = jnp.concatenate(
            [
                jnp.where(left, first, pltpu.roll(second, cap, 1)),
                jnp.where(left, pltpu.roll(first, cap, 1), second),
            ],
            axis=0,
        )
        return 0

    lax.fori_loop(0, slots // LANES, unpack, 0, unroll=16)
    field_ref[...] = jnp.zeros_like(field_ref)
    acc[...] = jnp.zeros_like(acc)
    depth = TILES * LANES
    outer = list(range(STEPS)) + list(range(lat_rows - STEPS, lat_rows))
    sides = list(range(STEPS)) + list(range(lon_cols - STEPS, lon_cols))

    def accumulate(t, _):
        data = rows[pl.ds(pl.multiple_of(t * depth, depth), depth), :]
        both = jnp.concatenate([meta[TILES * t + h] for h in range(TILES)], axis=1)
        col = column_hots(both, lon_cols)
        row = row_weights(both, 0, lat_rows)
        here = pl.ds(pl.multiple_of(t * depth, depth), depth)
        for k in range(4):
            hots_ref[k * lon_cols : (k + 1) * lon_cols, here] = col[k]
        rowb = [r.astype(BF16) for r in row]
        field_ref[...] += jnp.dot(spread_rows(col, row, outer, lon_cols), data, preferred_element_type=F32)
        parts = []
        for j in sides:
            total = None
            for k in range(4):
                same = jnp.where(both[4 + k : 5 + k] == float(j), 1.0, 0.0)
                term = jnp.broadcast_to(same, (lat_rows, depth)).astype(BF16) * rowb[k]
                total = term if total is None else total + term
            parts.append(total)
        acc[...] += jnp.dot(jnp.concatenate(parts, axis=0), data, preferred_element_type=F32)
        return 0

    lax.fori_loop(0, slots // depth, accumulate, 0)
    wide = STEPS * lon_cols
    strip_ref[...] = acc[...].astype(BF16)
    tmp[...] = jnp.zeros_like(tmp)
    for ref, first, at in ((south_ref, 0, 0), (north_ref, wide, lat_rows - STEPS)):
        tmp[0:STEPS, :] = rates_ref[at : at + STEPS, :]
        tmp[STEPS : 2 * STEPS, :] = rates_ref[lat_rows + at : lat_rows + at + STEPS, :]
        ref[:wide, :] = field_ref[first : first + wide, :].astype(BF16)
        ref[wide:, :] = tmp[...].astype(BF16)


def scatter_edges(recv, rates, devices, cap, lat_rows, lon_cols):
    slots = devices * cap
    full = pl.BlockSpec(memory_space=pltpu.VMEM)
    wide = STEPS * lon_cols
    shapes = [
        jax.ShapeDtypeStruct((slots, LANES), BF16),
        jax.ShapeDtypeStruct((slots // LANES, 16, LANES), F32),
        jax.ShapeDtypeStruct((4 * lon_cols, slots), BF16),
        jax.ShapeDtypeStruct((2 * wide, LANES), F32),
        jax.ShapeDtypeStruct((wide + 16, LANES), BF16),
        jax.ShapeDtypeStruct((wide + 16, LANES), BF16),
        jax.ShapeDtypeStruct((2 * STEPS * lat_rows, LANES), BF16),
    ]
    return pl.pallas_call(
        functools.partial(edge_kernel, cap, lat_rows, lon_cols),
        out_shape=shapes,
        in_specs=[full] * 2,
        out_specs=[full] * len(shapes),
        scratch_shapes=[pltpu.VMEM((2 * STEPS * lat_rows, LANES), F32), pltpu.VMEM((16, LANES), F32)],
        compiler_params=pltpu.CompilerParams(vmem_limit_bytes=24 * MIB),
        cost_estimate=pl.CostEstimate(flops=5_000_000_000, bytes_accessed=20_000_000, transcendentals=0),
        name="scatter_edges",
    )(recv, rates)


def middle_kernel(first, last, lon_cols, rows_ref, meta_ref, hots_ref, field_ref):
    field_ref[...] = jnp.zeros_like(field_ref)
    depth = MIDDLE_TILES * LANES
    per = 4

    def accumulate(t, _):
        data = rows_ref[pl.ds(pl.multiple_of(t * depth, depth), depth), :]
        both = jnp.concatenate([meta_ref[MIDDLE_TILES * t + h] for h in range(MIDDLE_TILES)], axis=1)
        here = pl.ds(pl.multiple_of(t * depth, depth), depth)
        col = [hots_ref[k * lon_cols : (k + 1) * lon_cols, here] for k in range(4)]
        row = row_weights(both, first, 16)
        for i in range(first, last, per):
            spread = spread_rows(col, row, range(i - first, i - first + per), lon_cols)
            at = pl.ds((i - first) * lon_cols, per * lon_cols)
            field_ref[at, :] += jnp.dot(spread, data, preferred_element_type=F32)
        return 0

    lax.fori_loop(0, rows_ref.shape[0] // depth, accumulate, 0)


def scatter_middle(rows, meta, hots, first, last, lon_cols):
    full = pl.BlockSpec(memory_space=pltpu.VMEM)
    return pl.pallas_call(
        functools.partial(middle_kernel, first, last, lon_cols),
        out_shape=jax.ShapeDtypeStruct(((last - first) * lon_cols, LANES), F32),
        in_specs=[full] * 3,
        out_specs=full,
        compiler_params=pltpu.CompilerParams(vmem_limit_bytes=20 * MIB),
        cost_estimate=pl.CostEstimate(flops=7_000_000_000, bytes_accessed=20_000_000, transcendentals=0),
        name="scatter_middle",
    )(rows, meta, hots)


def turn_kernel(lat_rows, lon_cols, below_ref, above_ref, strip_ref, rates_ref, west_ref, east_ref, tall_ref, cols, wide_rows):
    tall = lat_rows + 2 * STEPS
    wide = STEPS * lon_cols
    below = below_ref[...].astype(F32)
    above = above_ref[...].astype(F32)
    strip = strip_ref[...].astype(F32)
    wide_rows[0] = below
    wide_rows[1] = above
    for c in range(2):
        at = c * tall
        tall_ref[at : at + STEPS, :] = below[wide + c * STEPS : wide + (c + 1) * STEPS]
        tall_ref[at + STEPS : at + STEPS + lat_rows, :] = rates_ref[c * lat_rows : (c + 1) * lat_rows, :]
        tall_ref[at + STEPS + lat_rows : at + tall, :] = above[wide + c * STEPS : wide + (c + 1) * STEPS]
    for side, ref in ((0, west_ref), (1, east_ref)):
        first = side * (lon_cols // GROUPS - STEPS) * GROUPS + side * (GROUPS - 1)
        for j in range(STEPS):
            n = (side * STEPS + j) * lat_rows
            cols[pl.ds(STEPS * STEPS + j, lat_rows, stride=STEPS), :] = strip[n : n + lat_rows]
        for i in range(STEPS):
            picked = pl.ds(i * lon_cols + first, STEPS, stride=GROUPS)
            cols[pl.ds(STEPS * i, STEPS), :] = wide_rows[0, picked, :]
            cols[pl.ds(STEPS * (STEPS + lat_rows + i), STEPS), :] = wide_rows[1, picked, :]
        ref[: STEPS * tall, :] = cols[...].astype(BF16)
        ref[STEPS * tall :, :] = tall_ref[...].astype(BF16)


def turn(below, above, strip, rates, lat_rows, lon_cols):
    full = pl.BlockSpec(memory_space=pltpu.VMEM)
    tall = lat_rows + 2 * STEPS
    side = jax.ShapeDtypeStruct(((STEPS + 2) * tall, LANES), BF16)
    return pl.pallas_call(
        functools.partial(turn_kernel, lat_rows, lon_cols),
        out_shape=[side, side, jax.ShapeDtypeStruct((2 * tall, LANES), F32)],
        in_specs=[full] * 4,
        out_specs=[full] * 3,
        scratch_shapes=[pltpu.VMEM((STEPS * tall, LANES), F32), pltpu.VMEM((2, STEPS * lon_cols + 16, LANES), F32)],
        compiler_params=pltpu.CompilerParams(vmem_limit_bytes=3 * MIB),
        cost_estimate=pl.CostEstimate(flops=1_000_000, bytes_accessed=1_000_000, transcendentals=0),
        name="turn",
    )(below, above, strip, rates)


def diffuse_kernel(
    lat_rows,
    lon_cols,
    lat_devices,
    place_ref,
    outer_ref,
    mid1_ref,
    mid2_ref,
    below_ref,
    above_ref,
    west_ref,
    east_ref,
    rates_ref,
    gain_ref,
    jac_ref,
    out_hbm,
    out_ref,
    ping,
    pong,
    face_x,
    face_y,
    kappa,
    out_sems,
):
    width = lon_cols + 2 * PAD
    tall = lat_rows + 2 * STEPS
    lead = PAD - STEPS
    trail = PAD + lon_cols
    half = (lat_rows - 2 * STEPS) // 2
    part = lon_cols // GROUPS
    span = (part + 2 * STEPS) * GROUPS
    west = west_ref[...].astype(F32)
    east = east_ref[...].astype(F32)

    rest = jnp.zeros((LANES - tall, LANES), F32)
    for c in range(2):
        at = STEPS * tall + c * tall
        kappa[c, 0:lead, :] = jnp.zeros((lead, LANES), F32)
        kappa[c, lead:PAD, :] = jnp.concatenate([west[at : at + tall], rest], axis=0).T[LANES - STEPS :]
        kappa[c, PAD:trail, :] = jnp.concatenate([rates_ref[c * tall : (c + 1) * tall, :], rest], axis=0).T
        kappa[c, trail : trail + STEPS, :] = jnp.concatenate([east[at : at + tall], rest], axis=0).T[:STEPS]
        kappa[c, trail + STEPS :, :] = jnp.zeros((lead, LANES), F32)

    def strips(c):
        return jnp.concatenate(
            [kappa[c, pl.ds(lead + m, GROUPS, stride=part), :] for m in range(part + 2 * STEPS)], axis=0
        )

    kx, ky = strips(0), strips(1)
    ex = 0.5 * (kx + jnp.concatenate([kx[GROUPS:], kx[:GROUPS]], axis=0))
    row = place_ref[0] * lat_rows - STEPS + iota((span, LANES), 1)
    inside = (row >= 0) & (row < lat_rows * lat_devices - 1)
    ny = jnp.where(inside, 0.5 * (ky + pltpu.roll(ky, LANES - 1, 1)), 0.0)
    left = jnp.where(iota((2 * span, LANES), 1) < tall, jnp.concatenate([ex, ny], axis=0), 0.0)
    pieces = None
    for n in range(3):
        piece = left.astype(BF16).astype(F32)
        left = left - piece
        pieces = piece if n == 0 else pieces + pltpu.roll(piece, n * tall, 1)
    pieces = pieces.astype(BF16)
    lane = iota((LANES, LANES), 0) % tall
    for i in range(0, tall, 2):
        choice = jnp.concatenate([(lane == i).astype(F32), (lane == i + 1).astype(F32)], axis=1).astype(BF16)
        spread = jnp.dot(pieces, choice, preferred_element_type=F32)
        for u in range(2):
            at = pl.ds((i + u) * span, span)
            face_x[at, :] = spread[:span, u * LANES : (u + 1) * LANES]
            face_y[at, :] = spread[span:, u * LANES : (u + 1) * LANES]

    strip_id = iota((GROUPS, LANES), 0)
    inner = STEPS * GROUPS
    for i in range(tall):
        n = i - STEPS
        if n < 0:
            middle = below_ref[pl.ds(i * lon_cols, lon_cols), :].astype(F32)
        elif n < STEPS:
            middle = outer_ref[pl.ds(n * lon_cols, lon_cols), :]
        elif n < STEPS + half:
            middle = mid1_ref[pl.ds((n - STEPS) * lon_cols, lon_cols), :]
        elif n < STEPS + 2 * half:
            middle = mid2_ref[pl.ds((n - STEPS - half) * lon_cols, lon_cols), :]
        elif n < lat_rows:
            middle = outer_ref[pl.ds((n - 2 * half) * lon_cols, lon_cols), :]
        else:
            middle = above_ref[pl.ds((n - lat_rows) * lon_cols, lon_cols), :].astype(F32)
        ping[pl.ds(i * span + inner, lon_cols), :] = middle
        for q in range(STEPS):
            tail = middle[(part - STEPS + q) * GROUPS : (part - STEPS + q + 1) * GROUPS]
            side = jnp.broadcast_to(west[STEPS * i + q : STEPS * i + q + 1], (GROUPS, LANES))
            before = jnp.where(strip_id == 0, side, pltpu.roll(tail, 1, 0))
            ping[pl.ds(i * span + q * GROUPS, GROUPS), :] = before
            head = middle[q * GROUPS : (q + 1) * GROUPS]
            side = jnp.broadcast_to(east[STEPS * i + q : STEPS * i + q + 1], (GROUPS, LANES))
            after = jnp.where(strip_id == GROUPS - 1, side, pltpu.roll(head, GROUPS - 1, 0))
            ping[pl.ds(i * span + inner + lon_cols + q * GROUPS, GROUPS), :] = after

    for sweep in range(STEPS):
        old, new = (ping, pong) if sweep % 2 == 0 else (pong, ping)
        low, high = sweep + 1, tall - sweep - 1
        first, stop = sweep + 1, span // GROUPS - 1 - sweep
        cuts = [first + (stop - first) * n // SWEEP_PARTS for n in range(SWEEP_PARTS + 1)]
        for at, end in zip(cuts[:-1], cuts[1:]):
            inside_rows = (end - at) * GROUPS

            def load(ref, i, start, count):
                return ref[pl.ds(pl.multiple_of(i * span + start * GROUPS, 8), count), :]

            def one_row(i, carry, old=old, new=new, at=at, count=inside_rows):
                here, flux_below = carry
                above = load(old, i + 1, at - 1, count + 2 * GROUPS)
                flux_y = load(face_y, i, at, count) * (above - here)[GROUPS : count + GROUPS]
                flux_x = load(face_x, i, at - 1, count + GROUPS) * (here[GROUPS:] - here[: count + GROUPS])
                change = flux_x[GROUPS:] - flux_x[:count] + (flux_y - flux_below)
                new[pl.ds(pl.multiple_of(i * span + at * GROUPS, 8), count), :] = here[GROUPS : count + GROUPS] + change
                return above, flux_y

            here = load(old, low, at - 1, inside_rows + 2 * GROUPS)
            start = load(old, low - 1, at, inside_rows)
            start = load(face_y, low - 1, at, inside_rows) * (here[GROUPS : inside_rows + GROUPS] - start)
            lax.fori_loop(low, high, one_row, (here, start), unroll=UNROLL_SWEEP)

    last = ping if STEPS % 2 == 0 else pong
    gain = gain_ref[...]
    jac = jnp.concatenate([jac_ref[...], jac_ref[...]], axis=1)
    levels = jac_ref.shape[0]

    shape = out_hbm.shape
    stores = []
    band = lat_rows // OUT_PARTS
    for h in range(lat_rows // 2):
        pair = []
        for u in range(2):
            at = (2 * h + u + STEPS) * span + inner
            value = jnp.concatenate([last[pl.ds(at + t, part, stride=GROUPS), :] for t in range(GROUPS)], axis=0)
            value = value * gain
            head = value.astype(BF16)
            low = (value - head.astype(F32)).astype(BF16)
            pair.append(jnp.concatenate([head, low], axis=1))
        both = jnp.concatenate(pair, axis=0)
        result = lax.dot_general(jac, both, (((1,), (1,)), ((), ())), preferred_element_type=F32)
        out_ref[pl.ds(2 * h, levels, stride=lat_rows), :] = result[:, :lon_cols]
        out_ref[pl.ds(2 * h + 1, levels, stride=lat_rows), :] = result[:, lon_cols:]
        if (2 * h + 2) % band == 0:
            rows = pl.ds(2 * h + 2 - band, band)
            n = len(stores)
            stores.append(
                pltpu.make_async_copy(out_ref.reshape(shape).at[:, rows, :], out_hbm.at[:, rows, :], out_sems.at[n])
            )
            stores[n].start()
    for store in stores:
        store.wait()


def diffuse(place, outer, mid1, mid2, below, above, west, east, rates, inv_var, jacobian, lat_rows, lon_cols, lats):
    full = pl.BlockSpec(memory_space=pltpu.VMEM)
    levels = jacobian.shape[1]
    tall, width = lat_rows + 2 * STEPS, lon_cols + 2 * PAD
    span = lon_cols + 2 * STEPS * GROUPS
    return pl.pallas_call(
        functools.partial(diffuse_kernel, lat_rows, lon_cols, lats),
        out_shape=jax.ShapeDtypeStruct((levels, lat_rows, lon_cols), F32),
        in_specs=[pl.BlockSpec(memory_space=pltpu.SMEM)] + [full] * 10,
        out_specs=pl.BlockSpec(memory_space=pltpu.HBM),
        scratch_shapes=[pltpu.VMEM((levels * lat_rows, lon_cols), F32)]
        + [pltpu.VMEM((tall * span, LANES), F32)] * 4
        + [pltpu.VMEM((2, width, LANES), F32), pltpu.SemaphoreType.DMA((OUT_PARTS,))],
        compiler_params=pltpu.CompilerParams(vmem_limit_bytes=28 * MIB),
        cost_estimate=pl.CostEstimate(flops=1_000_000_000, bytes_accessed=20_000_000, transcendentals=0),
        name="diffuse",
    )(place, outer, mid1, mid2, below, above, west, east, rates, inv_var.reshape(1, -1), jacobian.T)


def moved(value, axis, step, wrap):
    size = lax.axis_size(axis)
    pairs = [((i + step) % size, i) for i in range(size) if wrap or 0 <= i + step < size]
    return lax.ppermute(value, axis, pairs)


def local(departures, obs_owner, obs_cells, interp_weights, inv_var, jacobian, face_rates):
    devices = lax.axis_size(("lon", "lat"))
    cap = 2 * departures.shape[0] // devices
    lat_rows, lon_cols = face_rates.shape[1:]
    rates = face_rates.reshape(2 * lat_rows, lon_cols)
    send = pack(obs_owner, obs_cells, interp_weights, departures, devices, cap)
    recv = lax.all_to_all(
        send.reshape(devices, cap + META, LANES), ("lon", "lat"), split_axis=0, concat_axis=0, tiled=True
    ).reshape(devices * (cap + META), LANES)
    rows, meta, hots, outer, south, north, strip = scatter_edges(recv, rates, devices, cap, lat_rows, lon_cols)
    below = moved(north, "lat", -1, False)
    above = moved(south, "lat", 1, False)
    middle = lat_rows // 2
    mid1 = scatter_middle(rows, meta, hots, STEPS, middle, lon_cols)
    meta, below, above = lax.optimization_barrier((meta, below, above))
    to_west, to_east, tall_rates = turn(below, above, strip, rates, lat_rows, lon_cols)
    west = moved(to_east, "lon", -1, True)
    east = moved(to_west, "lon", 1, True)
    mid2 = scatter_middle(rows, meta, hots, middle, lat_rows - STEPS, lon_cols)
    place = lax.axis_index("lat").astype(jnp.int32).reshape(1)
    return diffuse(
        place,
        outer,
        mid1,
        mid2,
        below,
        above,
        west,
        east,
        tall_rates,
        inv_var,
        jacobian,
        lat_rows,
        lon_cols,
        lax.axis_size("lat"),
    )


def solution(mesh):
    in_specs = (
        P(("lon", "lat"), None),
        P(("lon", "lat"), None),
        P(("lon", "lat"), None),
        P(("lon", "lat"), None),
        P(),
        P(),
        P(None, "lat", "lon"),
    )
    out_specs = P(None, "lat", "lon")
    return jax.shard_map(local, mesh=mesh, in_specs=in_specs, out_specs=out_specs, check_vma=False)
```
